32 devices in a mesh: gx: 16 (over z, x, core), gy: 2 (over y).
Axes of the slice: x: 2, y: 2, z: 4, core: 2. Of those that a mesh axis runs over, the one named last changes fastest.
Arguments:
- field: float32 [32, 64, 32, 256], P(None, 'gx', 'gy'), may hold values from -6 to 6
- spec_weight: float32 [2, 32, 32, 32, 32, 32], P(None, None, 'gx', 'gy'), may hold values from -3 to 3
- dw_kernel: float32 [32, 3, 3, 3], replicated, may hold values from -1.25 to 1.25
- point_weight: float32 [32, 32], replicated, may hold values from -1 to 1
- bias: float32 [32], replicated, may hold values from -3 to 3
Outputs:
- evolved: float32 [32, 64, 32, 256], P(None, 'gx', 'gy')
The draws below stay inside these ranges and needn't reach their ends.
All inputs are finite; a program needn't handle non-finite values.
Results may differ from the reference program's by a relative error of at most 0.00005.
Values sent between devices are 32-bit elements; how exact they have to be, the bound alone decides.
A program may use at most 256 MiB of HBM per device.

```python
import jax
import jax.numpy as jnp
from jax import lax

C = 32
MODES = 32
NZ = 256
NX = 64
NY = 32


def steps_of(own_key, extent, pieces, smallest, top_value):
    gain, own = 1.0, jax.random.fold_in(own_key, 6)
    for axis_at, shards_of in pieces:
        steps = jnp.exp(jax.random.uniform(jax.random.fold_in(own, axis_at), (shards_of,), jnp.float32, smallest / len(pieces), top_value / len(pieces)))
        gain = gain * jnp.repeat(steps, extent[axis_at] // shards_of).reshape([-1 if axis == axis_at else 1 for axis in range(len(extent))])
    return gain


def noise(stream_key, dims, spread, bound, split=(), kind=jnp.bfloat16):
    drawn = spread * jax.random.normal(stream_key, dims, jnp.float32)
    if split:
        drawn = drawn * steps_of(stream_key, dims, split, -0.22, 0.18)
    return jnp.clip(drawn, -bound, bound).astype(kind)


def setup_inputs(seed: int = 0) -> dict:
    key_of = jax.random.split(jax.random.key(seed), 6)
    return {
        "field": noise(key_of[0], (C, NX, NY, NZ), 1.0, 6.0, ((1, 16), (2, 2)), jnp.float32),
        "spec_weight": noise(key_of[1], (2, MODES, MODES, MODES, C, C), (max(1, 2 * C * MODES**3 // (NX * NY * NZ))) ** -0.5, 3.0, ((2, 16), (3, 2)), jnp.float32),
        "dw_kernel": noise(key_of[2], (C, 3, 3, 3), 27 ** -0.5, 1.25, (), jnp.float32),
        "point_weight": noise(key_of[3], (C, C), C ** -0.5, 1.0, (), jnp.float32),
        "bias": noise(key_of[4], (C,), 0.5, 3.0, (), jnp.float32),
    }


def truncate(values, axis, length):
    half = MODES // 2
    low = lax.slice_in_dim(values, 0, half, axis=axis)
    high = lax.slice_in_dim(values, length - half, length, axis=axis)
    return jnp.concatenate([low, high], axis=axis)


def widen(values, axis, length):
    half = MODES // 2
    low = lax.slice_in_dim(values, 0, half, axis=axis)
    high = lax.slice_in_dim(values, half, MODES, axis=axis)
    shape = list(values.shape)
    shape[axis] = length - MODES
    return jnp.concatenate([low, jnp.zeros(shape, values.dtype), high], axis=axis)


def reference(field, spec_weight, dw_kernel, point_weight, bias):
    exact_mode = lax.Precision.HIGHEST
    zspec = jnp.fft.rfft(field, axis=3)[..., :MODES]
    yspec = truncate(jnp.fft.fft(zspec, axis=2), 2, NY)
    xspec = truncate(jnp.fft.fft(yspec, axis=1), 1, NX)
    real_in = jnp.real(xspec).astype(jnp.float32)
    imag_in = jnp.imag(xspec).astype(jnp.float32)
    weight_re = spec_weight[0].astype(jnp.float32)
    weight_im = spec_weight[1].astype(jnp.float32)
    pattern = "ixyz,xyzio->oxyz"
    out_re = jnp.einsum(pattern, real_in, weight_re, precision=exact_mode) - jnp.einsum(pattern, imag_in, weight_im, precision=exact_mode)
    out_im = jnp.einsum(pattern, real_in, weight_im, precision=exact_mode) + jnp.einsum(pattern, imag_in, weight_re, precision=exact_mode)
    mixed = out_re + 1j * out_im
    back_x = jnp.fft.ifft(widen(mixed, 1, NX), axis=1)
    back_y = jnp.fft.ifft(widen(back_x, 2, NY), axis=2)
    tail = jnp.zeros(back_y.shape[:3] + (NZ // 2 + 1 - MODES,), back_y.dtype)
    spectral = jnp.fft.irfft(jnp.concatenate([back_y, tail], axis=3), n=NZ, axis=3).astype(jnp.float32)
    padded = jnp.pad(field, ((0, 0), (1, 1), (1, 1), (1, 1)), mode="wrap")
    conv = jnp.zeros(field.shape, jnp.float32)
    for shift_x in range(3):
        for shift_y in range(3):
            for shift_z in range(3):
                tap = dw_kernel[:, shift_x, shift_y, shift_z][:, None, None, None]
                conv = conv + tap * padded[:, shift_x:shift_x + NX, shift_y:shift_y + NY, shift_z:shift_z + NZ]
    pointwise = jnp.einsum("ixyz,io->oxyz", field, point_weight, precision=exact_mode)
    total = spectral + conv + pointwise + bias[:, None, None, None]
    return jax.nn.gelu(total)
```

```python
import functools

import jax
import jax.numpy as jnp
import numpy as np
from jax import lax
from jax.experimental import pallas as pl
from jax.experimental.pallas import tpu as pltpu
from jax.sharding import PartitionSpec as P

EXACT = lax.Precision.HIGHEST
MIB = 1 << 20


def params(mib, **more):
    return pltpu.CompilerParams(vmem_limit_bytes=mib * MIB, **more)


def dot(a, b, dims=((1,), (0,))):
    return lax.dot_general(a, b, (dims, ((), ())), precision=EXACT, preferred_element_type=jnp.float32)


def kept(modes, length):
    index = np.arange(modes)
    return np.where(index < modes // 2, index, index + length - modes)


def waves(freqs, length):
    angle = (freqs[:, None] * np.arange(length)[None, :] % length) * (2.0 * np.pi / length)
    return np.cos(angle), np.sin(angle)


def table_z(modes, depth, groups):
    cosine, sine = waves(np.arange(modes), depth)
    kl = modes // groups
    both = np.stack([cosine, -sine]).reshape(2, groups, kl, depth)
    return both.transpose(1, 0, 2, 3).reshape(2 * modes, depth).astype(np.float32)


def table_z_back(modes, depth, groups):
    cosine, sine = waves(np.arange(modes), depth)
    weight = (np.where(np.arange(modes) == 0, 1.0, 2.0) / depth)[:, None]
    kl = modes // groups
    both = np.stack([weight * cosine, -weight * sine]).reshape(2, groups, kl, depth)
    return both.transpose(1, 0, 2, 3).reshape(2 * modes, depth).astype(np.float32)


def table_pair(modes, length, direction):
    cosine, sine = waves(kept(modes, length), length)
    upper = np.stack([cosine, direction * sine])
    lower = np.stack([-direction * sine, cosine])
    return np.stack([upper, lower])


def z_kernel(table_ref, field_ref, out_ref):
    rows, lanes = field_ref.shape[0], out_ref.shape[-1]
    spec = dot(table_ref[...], field_ref[...], ((1,), (1,)))
    groups, count, part, _ = out_ref.shape
    for g in range(groups):
        for y in range(count):
            out_ref[g, y] = spec[g * part : (g + 1) * part, y * lanes : (y + 1) * lanes]


def y_kernel(kl, table_ref, in_ref, out_ref):
    full_y = in_ref.shape[0] // (2 * kl)
    lanes = in_ref.shape[1]
    parts = []
    for k in range(kl):
        parts.append(jnp.concatenate([in_ref[pl.ds(r * kl + k, full_y, stride=2 * kl), :] for r in range(2)], axis=0))
    spec = dot(table_ref[...], jnp.concatenate(parts, axis=1))
    rows = spec.shape[0]
    for k in range(kl):
        out_ref[pl.ds(k, rows, stride=kl), :] = spec[:, k * lanes : (k + 1) * lanes]


def y_back_kernel(kl, table_ref, in_ref, out_ref):
    lanes = in_ref.shape[1]
    rows_in = in_ref.shape[0] // kl
    data = jnp.concatenate([in_ref[pl.ds(k, rows_in, stride=kl), :] for k in range(kl)], axis=1)
    spec = dot(table_ref[...], data)
    rows = spec.shape[0]
    for k in range(kl):
        out_ref[pl.ds(k, rows, stride=kl), :] = spec[:, k * lanes : (k + 1) * lanes]


def mix_kernel(cfg, fwd_ref, back_ref, in_ref, weight_ref, out_ref, held):
    owners, nlc, kl, rx, modes, chans = cfg
    kb = weight_ref.shape[3]
    nl = pl.program_id(0)
    lanes = rx * chans
    stride = nlc * 2 * kl
    held[...] = jnp.zeros_like(held)
    for kk in range(kb):
        k = pl.program_id(1) * kb + kk
        data = jnp.concatenate(
            [in_ref[pl.ds((nl * 2 + s) * kl + k, owners, stride=stride), :] for s in range(2)], axis=0
        )
        wide = dot(data, fwd_ref[...], ((0,), (0,)))
        spec = wide[:chans, :128]
        for x in range(1, rx):
            spec = spec + wide[x * chans : (x + 1) * chans, x * 128 : (x + 1) * 128]
        for m in range(modes):
            re = jnp.broadcast_to(spec[:, m : m + 1], (chans, chans))
            im = jnp.broadcast_to(spec[:, modes + m : modes + m + 1], (chans, chans))
            wre = weight_ref[0, m, 0, kk]
            wim = weight_ref[1, m, 0, kk]
            held[m : m + 1, :chans] = jnp.sum(re * wre - im * wim, axis=0, keepdims=True)
            held[modes + m : modes + m + 1, :chans] = jnp.sum(re * wim + im * wre, axis=0, keepdims=True)
        mixed = held[...]
        turned = [mixed] + [pltpu.roll(mixed, x * chans, 1) for x in range(1, rx)]
        back = dot(back_ref[...], jnp.concatenate(turned, axis=0))
        for s in range(2):
            out_ref[pl.ds((nl * 2 + s) * kl + k, owners, stride=stride), :] = back[s * owners : (s + 1) * owners]


def last_kernel(ztab_ref, taps_ref, point_ref, bias_ref, spec_ref, field_ref, xlo_ref, xhi_ref, ylo_ref, yhi_ref,
                out_ref, pad, base, sems):
    rows_y, rx, chans, depth = field_ref.shape
    y = pl.program_id(0)

    @pl.when(y == 0)
    def _():
        copies = [
            pltpu.make_async_copy(field_ref, pad.at[pl.ds(1, rows_y), pl.ds(1, rx)], sems.at[0]),
            pltpu.make_async_copy(xlo_ref, pad.at[pl.ds(1, rows_y), pl.ds(0, 1)], sems.at[1]),
            pltpu.make_async_copy(xhi_ref, pad.at[pl.ds(1, rows_y), pl.ds(rx + 1, 1)], sems.at[2]),
            pltpu.make_async_copy(ylo_ref, pad.at[pl.ds(0, 1)], sems.at[3]),
            pltpu.make_async_copy(yhi_ref, pad.at[pl.ds(rows_y + 1, 1)], sems.at[4]),
        ]
        for copy in copies:
            copy.start()
        for copy in copies:
            copy.wait()

    groups, _, part, lanes = spec_ref.shape
    spectra = spec_ref[...].reshape(groups * part, lanes)
    here = pad[y + 1, pl.ds(1, rx)].reshape(rx * chans, depth)
    base[...] = dot(spectra, ztab_ref[...], ((0,), (0,))) + dot(point_ref[...], here)
    for cc in range(0, chans, 8):
        sums = [[None] * 3 for _ in range(rx)]
        for b in range(3):
            for xp in range(rx + 2):
                value = pad[y + b, xp, cc : cc + 8, :]
                for a in range(3):
                    x = xp - a
                    if 0 <= x < rx:
                        for e in range(3):
                            tap = taps_ref[(a * 3 + b) * 3 + e, cc : cc + 8, :]
                            term = jnp.concatenate([tap] * (depth // 128), axis=1) * value
                            sums[x][e] = term if sums[x][e] is None else sums[x][e] + term
        for x in range(rx):
            total = sums[x][1] + pltpu.roll(sums[x][0], 1, 1) + pltpu.roll(sums[x][2], depth - 1, 1)
            total = total + base[x * chans + cc : x * chans + cc + 8, :]
            bias = bias_ref[cc : cc + 8, :]
            v = total + jnp.concatenate([bias] * (depth // 128), axis=1)
            inner = np.float32(np.sqrt(2.0 / np.pi)) * (v + np.float32(0.044715) * (v * v * v))
            out_ref[0, x, cc : cc + 8, :] = 0.5 * v * (1.0 + jnp.tanh(inner))


def on_device(field, spec_weight, dw_kernel, point_weight, bias):
    gx, gy = lax.axis_size("gx"), lax.axis_size("gy")
    chans, rx, ry, depth = field.shape
    modes, nlc, kl = spec_weight.shape[1:4]
    full_x, full_y = rx * gx, ry * gy
    lanes = rx * chans
    f32 = jnp.float32

    cells = jnp.transpose(field, (2, 1, 0, 3))
    ring = lambda n: [(i, (i + 1) % n) for i in range(n)]
    back_ring = lambda n: [(j, i) for i, j in ring(n)]
    xlo = lax.ppermute(cells[:, rx - 1 :], "gx", ring(gx))
    xhi = lax.ppermute(cells[:, :1], "gx", back_ring(gx))
    edge = lambda at: jnp.concatenate([xlo[at : at + 1], cells[at : at + 1], xhi[at : at + 1]], axis=1)
    ylo = lax.ppermute(edge(ry - 1), "gy", ring(gy))
    yhi = lax.ppermute(edge(0), "gy", back_ring(gy))

    zspec = pl.pallas_call(
        z_kernel,
        out_shape=jax.ShapeDtypeStruct((gy, ry, 2 * kl, lanes), f32),
        compiler_params=params(32),
        name="z_forward",
    )(table_z(modes, depth, gy), cells.reshape(ry * lanes, depth))
    wide = lax.all_to_all(zspec, "gy", split_axis=0, concat_axis=0, tiled=True)

    ytab = table_pair(modes, full_y, 1.0).transpose(2, 0, 1, 3).reshape(2 * modes, 2 * full_y).astype(np.float32)
    yspec = pl.pallas_call(
        functools.partial(y_kernel, kl),
        out_shape=jax.ShapeDtypeStruct((2 * modes * kl, lanes), f32),
        compiler_params=params(32),
        name="y_forward",
    )(ytab, wide.reshape(full_y * 2 * kl, lanes))
    columns = lax.all_to_all(yspec, "gx", split_axis=0, concat_axis=0, tiled=True)

    xtab = table_pair(modes, full_x, 1.0).reshape(2, 2, modes, gx, rx)
    fwd = np.zeros((2, gx, rx, 128), np.float32)
    fwd[..., : 2 * modes] = xtab.transpose(1, 3, 4, 0, 2).reshape(2, gx, rx, 2 * modes)
    fwd = fwd.reshape(2 * gx, rx * 128)
    xback = (table_pair(modes, full_x, -1.0) / full_x).reshape(2, 2, modes, gx, rx)
    back = xback.transpose(0, 3, 4, 1, 2).reshape(2 * gx, rx * 2 * modes).astype(np.float32)
    kb = 2
    mixed = pl.pallas_call(
        functools.partial(mix_kernel, (gx, nlc, kl, rx, modes, chans)),
        grid=(nlc, kl // kb),
        in_specs=[
            pl.BlockSpec(fwd.shape, lambda i, j: (0, 0)),
            pl.BlockSpec(back.shape, lambda i, j: (0, 0)),
            pl.BlockSpec((2 * modes * kl, lanes), lambda i, j: (0, 0)),
            pl.BlockSpec((2, modes, 1, kb, chans, chans), lambda i, j: (0, 0, i, j, 0, 0)),
        ],
        out_specs=pl.BlockSpec((2 * modes * kl, lanes), lambda i, j: (0, 0)),
        out_shape=jax.ShapeDtypeStruct((2 * modes * kl, lanes), f32),
        scratch_shapes=[pltpu.VMEM((2 * modes, 128), f32)],
        compiler_params=params(40),
        name="x_mix_x",
    )(fwd, back, columns, spec_weight)
    returned = lax.all_to_all(mixed, "gx", split_axis=0, concat_axis=0, tiled=True)

    yback = (table_pair(modes, full_y, -1.0) / full_y).transpose(3, 0, 2, 1)
    yback = yback.reshape(2 * full_y, 2 * modes).astype(np.float32)
    tall = pl.pallas_call(
        functools.partial(y_back_kernel, kl),
        out_shape=jax.ShapeDtypeStruct((2 * full_y * kl, lanes), f32),
        compiler_params=params(32),
        name="y_backward",
    )(yback, returned)
    spectra = lax.all_to_all(tall.reshape(gy, ry, 2 * kl, lanes), "gy", split_axis=0, concat_axis=0, tiled=True)

    taps = jnp.broadcast_to(dw_kernel.reshape(chans, 27).T[:, :, None], (27, chans, 128))
    point = jnp.kron(jnp.eye(rx, dtype=f32), point_weight.T)
    biases = jnp.broadcast_to(bias[:, None], (chans, 128))
    ztab = table_z_back(modes, depth, gy)
    whole = lambda a: pl.BlockSpec(a.shape, lambda i: (0,) * a.ndim)
    hbm = pl.BlockSpec(memory_space=pl.ANY)
    out = pl.pallas_call(
        last_kernel,
        grid=(ry,),
        in_specs=[whole(ztab), whole(taps), whole(point), whole(biases),
                  pl.BlockSpec((gy, 1, 2 * kl, lanes), lambda i: (0, i, 0, 0)), hbm, hbm, hbm, hbm, hbm],
        out_specs=pl.BlockSpec((1, rx, chans, depth), lambda i: (i, 0, 0, 0)),
        out_shape=jax.ShapeDtypeStruct((ry, rx, chans, depth), f32),
        scratch_shapes=[
            pltpu.VMEM((ry + 2, rx + 2, chans, depth), f32),
            pltpu.VMEM((lanes, depth), f32),
            pltpu.SemaphoreType.DMA((5,)),
        ],
        compiler_params=params(32),
        name="conv_point_gelu",
    )(ztab, taps, point, biases, spectra, cells, xlo, xhi, ylo, yhi)
    return jnp.transpose(out, (2, 1, 0, 3))


def solution(mesh):
    placed = (P(None, "gx", "gy", None), P(None, None, "gx", "gy", None, None), P(), P(), P())
    return jax.shard_map(
        on_device, mesh=mesh, in_specs=placed, out_specs=P(None, "gx", "gy", None), check_vma=False
    )
```

```python
import functools

import jax
import jax.numpy as jnp
import numpy as np
from jax import lax
from jax.experimental import pallas as pl
from jax.experimental.pallas import tpu as pltpu
from jax.sharding import PartitionSpec as P

EXACT = lax.Precision.HIGHEST
MIB = 1 << 20


def params(mib, **more):
    return pltpu.CompilerParams(vmem_limit_bytes=mib * MIB, **more)


def dot(a, b, dims=((1,), (0,))):
    return lax.dot_general(a, b, (dims, ((), ())), precision=EXACT, preferred_element_type=jnp.float32)


def kept(modes, length):
    index = np.arange(modes)
    return np.where(index < modes // 2, index, index + length - modes)


def waves(freqs, length):
    angle = (freqs[:, None] * np.arange(length)[None, :] % length) * (2.0 * np.pi / length)
    return np.cos(angle), np.sin(angle)


def table_pair(modes, length, direction):
    cosine, sine = waves(kept(modes, length), length)
    upper = np.stack([cosine, direction * sine])
    lower = np.stack([-direction * sine, cosine])
    return np.stack([upper, lower])


def rows_z(modes, depth, groups, pieces, table):
    kc = modes // (groups * pieces)
    return table.reshape(2, groups, pieces, kc, depth).transpose(2, 1, 0, 3, 4).reshape(2 * modes, depth).astype(np.float32)


def tables(cfg):
    gx, gy, rx, ry, depth, modes, pieces = cfg
    full_x, full_y = rx * gx, ry * gy
    cosine, sine = waves(np.arange(modes), depth)
    zfwd = rows_z(modes, depth, gy, pieces, np.stack([cosine, -sine]))
    weight = (np.where(np.arange(modes) == 0, 1.0, 2.0) / depth)[:, None]
    zback = rows_z(modes, depth, gy, pieces, np.stack([weight * cosine, -weight * sine]))
    yfwd = table_pair(modes, full_y, 1.0).transpose(2, 0, 1, 3).reshape(2 * modes, 2 * full_y).astype(np.float32)
    yback = (table_pair(modes, full_y, -1.0) / full_y).transpose(3, 0, 2, 1)
    yback = yback.reshape(2 * full_y, 2 * modes).astype(np.float32)
    xtab = table_pair(modes, full_x, 1.0).reshape(2, 2, modes, gx, rx).transpose(4, 1, 3, 0, 2)
    xfwd = np.zeros((rx, 4, 2, gx, 4, 2, modes), np.float32)
    for j in range(4):
        xfwd[:, j, :, :, j] = xtab
    xfwd = xfwd.reshape(rx * 8 * gx, 8 * modes)
    xback = (table_pair(modes, full_x, -1.0) / full_x).reshape(2, 2, modes, gx, rx)
    xback = xback.transpose(4, 0, 3, 1, 2).reshape(rx * 2 * gx, 2 * modes)
    xback = np.repeat(xback, 8, axis=1).astype(np.float32)
    return zfwd, yfwd, xfwd, xback, yback, zback


def layer_kernel(cfg, zfwd, yfwd, xfwd, xback, yback, zback, taps, point, biases, cells, weight_hbm, out,
                 weight, pad, zs, zr, ys, yr, ms, mr, ts, tr, spec, parts,
                 wsem, zss, zrs, yss, yrs, mss, mrs, tss, trs, hss, hrs):
    gx, gy, rx, ry, depth, modes, pieces = cfg
    chans = cells.shape[2]
    lanes = rx * chans
    full_y = ry * gy
    nlc, kl = weight.shape[2:4]
    kc = kl // pieces
    quads = kc // 4
    groups = nlc * quads
    xblk = nlc * 2 * kc
    yblk = ry * 2 * kc
    mx, my = lax.axis_index("gx"), lax.axis_index("gy")
    MESH = pl.DeviceIdType.MESH

    def weight_copy(p):
        at = pl.ds(p * kc, kc)
        return pltpu.make_async_copy(weight_hbm.at[:, :, :, at], weight.at[:, :, :, at], wsem.at[p])

    for p in range(pieces):
        weight_copy(p).start()

    barrier = pltpu.get_barrier_semaphore()
    for d in range(1, gx):
        pl.semaphore_signal(barrier, inc=1, device_id=(lax.rem(mx + d, gx), my), device_id_type=MESH)
    for d in range(1, gy):
        pl.semaphore_signal(barrier, inc=1, device_id=(mx, lax.rem(my + d, gy)), device_id_type=MESH)

    def block(ref, p, at, rows):
        return ref.at[p, pl.ds(pl.multiple_of(at * rows, 8), rows)]

    def xcopy(src, dst, ssem, rsem, p, d):
        to = lax.rem(mx + d, gx)
        return pltpu.make_async_remote_copy(
            src_ref=block(src, p, to, xblk), dst_ref=block(dst, p, mx, xblk), send_sem=ssem.at[p, to],
            recv_sem=rsem.at[p, mx], device_id=(to, my), device_id_type=MESH)

    def xarrived(src, dst, ssem, rsem, p, d):
        of = lax.rem(mx + d, gx)
        return pltpu.make_async_remote_copy(
            src_ref=block(src, p, of, xblk), dst_ref=block(dst, p, of, xblk), send_sem=ssem.at[p, of],
            recv_sem=rsem.at[p, of], device_id=(of, my), device_id_type=MESH)

    def ycopy(src, dst, ssem, rsem, p, d):
        to = lax.rem(my + d, gy)
        return pltpu.make_async_remote_copy(
            src_ref=block(src, p, to, yblk), dst_ref=block(dst, p, my, yblk), send_sem=ssem.at[p, to],
            recv_sem=rsem.at[p, my], device_id=(mx, to), device_id_type=MESH)

    def yarrived(src, dst, ssem, rsem, p, d):
        of = lax.rem(my + d, gy)
        return pltpu.make_async_remote_copy(
            src_ref=block(src, p, of, yblk), dst_ref=block(dst, p, of, yblk), send_sem=ssem.at[p, of],
            recv_sem=rsem.at[p, of], device_id=(mx, of), device_id_type=MESH)

    def each(make, act, count, *args):
        def step(d, carry):
            act(make(*args, d))
            return carry
        lax.fori_loop(1, count, step, 0)

    start, sent, got = lambda c: c.start(), lambda c: c.wait_send(), lambda c: c.wait_recv()
    zargs, yargs = (zs, zr, zss, zrs), (ys, yr, yss, yrs)
    margs, targs = (ms, mr, mss, mrs), (ts, tr, tss, trs)

    def keep_own(src, dst, p, at, rows):
        own = pl.ds(pl.multiple_of(at * rows, 8), rows)
        dst[p, own, :] = src[p, own, :]

    def halo(i):
        if i < 2:
            to = lax.rem(mx + (1 if i == 0 else gx - 1), gx)
            src = cells.at[:, pl.ds(rx - 1 if i == 0 else 0, 1)]
            dst = pad.at[pl.ds(1, ry), pl.ds(0 if i == 0 else rx + 1, 1)]
            where = (to, my)
        else:
            to = lax.rem(my + (1 if i == 2 else gy - 1), gy)
            src = pad.at[pl.ds(ry if i == 2 else 1, 1)]
            dst = pad.at[pl.ds(0 if i == 2 else ry + 1, 1)]
            where = (mx, to)
        return pltpu.make_async_remote_copy(
            src_ref=src, dst_ref=dst, send_sem=hss.at[i], recv_sem=hrs.at[i], device_id=where, device_id_type=MESH)

    zspec = dot(zfwd[...], cells[...].reshape(ry * lanes, depth), ((1,), (1,)))
    for p in range(pieces):
        for g in range(gy):
            for y in range(ry):
                at = (p * gy + g) * 2 * kc
                row = (g * ry + y) * 2 * kc
                zs[p, row : row + 2 * kc, :] = zspec[at : at + 2 * kc, y * lanes : (y + 1) * lanes]

    pl.semaphore_wait(barrier, gx + gy - 2)
    for p in range(pieces):
        each(ycopy, start, gy, *zargs, p)
    halo(0).start()
    halo(1).start()

    def inner(y, carry):
        pad[y + 1, pl.ds(1, rx)] = cells[y]
        return carry

    lax.fori_loop(0, ry, inner, 0)

    for p in range(pieces):
        keep_own(zs, zr, p, my, yblk)
        each(yarrived, got, gy, *zargs, p)
        data = jnp.concatenate([
            jnp.concatenate([zr[p, pl.ds(r * kc + k, full_y, stride=2 * kc), :] for r in range(2)], axis=0)
            for k in range(kc)], axis=1)
        yspec = dot(yfwd[...], data)
        for k in range(kc):
            ys[p, pl.ds(k, 2 * modes, stride=kc), :] = yspec[:, k * lanes : (k + 1) * lanes]
        each(xcopy, start, gx, *yargs, p)
        keep_own(ys, yr, p, mx, xblk)

    halo(0).wait_recv()
    halo(1).wait_recv()
    halo(2).start()
    halo(3).start()

    def local_part(y, carry):
        here = pad[y + 1, pl.ds(1, rx)].reshape(lanes, depth)
        base = dot(point[...], here)
        for cc in range(0, chans, 8):
            sums = [[None] * 3 for _ in range(rx)]
            for b in range(3):
                for xp in range(rx + 2):
                    value = pad[y + b, xp, cc : cc + 8, :]
                    for a in range(3):
                        x = xp - a
                        if 0 <= x < rx:
                            for e in range(3):
                                tap = taps[(a * 3 + b) * 3 + e, cc : cc + 8, :]
                                term = jnp.concatenate([tap] * (depth // 128), axis=1) * value
                                sums[x][e] = term if sums[x][e] is None else sums[x][e] + term
            bias = jnp.concatenate([biases[cc : cc + 8, :]] * (depth // 128), axis=1)
            for x in range(rx):
                total = sums[x][1] + pltpu.roll(sums[x][0], 1, 1) + pltpu.roll(sums[x][2], depth - 1, 1)
                out[y, x, cc : cc + 8, :] = total + base[x * chans + cc : x * chans + cc + 8, :] + bias
        return carry

    lax.fori_loop(1, ry // 2, local_part, 0)

    for p in range(pieces):
        each(xarrived, got, gx, *yargs, p)
        gathered = []
        for g in range(groups):
            nl, q = g // quads, g % quads
            data = jnp.concatenate(
                [yr[p, pl.ds((nl * 2 + s) * kc + q * 4 + j, gx, stride=xblk), :] for j in range(4) for s in range(2)],
                axis=0)
            turned = data.T
            gathered.append(jnp.concatenate([turned[x * chans : (x + 1) * chans] for x in range(rx)], axis=1))
        spec[...] = dot(jnp.concatenate(gathered, axis=0), xfwd[...])
        weight_copy(p).wait()

        def mix(g, carry):
            nl, q = g // quads, g % quads
            at = pl.ds(pl.multiple_of(g * chans, 8), chans)
            for m in range(modes):
                res, ims = [], []
                for j in range(4):
                    lane = j * 2 * modes + m
                    half = spec[at, j * 2 * modes // 128 * 128 : j * 2 * modes // 128 * 128 + 128]
                    lane = lane % 128
                    re = jnp.broadcast_to(half[:, lane : lane + 1], (chans, chans))
                    im = jnp.broadcast_to(half[:, lane + modes : lane + modes + 1], (chans, chans))
                    wre = weight[0, m, nl, p * kc + q * 4 + j]
                    wim = weight[1, m, nl, p * kc + q * 4 + j]
                    mre = re * wre - im * wim
                    mim = re * wim + im * wre
                    res.append(sum(mre[i : i + 8] for i in range(8, chans, 8)) + mre[:8])
                    ims.append(sum(mim[i : i + 8] for i in range(8, chans, 8)) + mim[:8])
                parts[g, m * 8 : m * 8 + 8, :] = jnp.concatenate(res, axis=1)
                parts[g, (modes + m) * 8 : (modes + m) * 8 + 8, :] = jnp.concatenate(ims, axis=1)
            return carry

        lax.fori_loop(0, groups, mix, 0)
        back = dot(xback[...], jnp.concatenate([parts[g] for g in range(groups)], axis=1))
        for g in range(groups):
            nl, q = g // quads, g % quads
            for j in range(4):
                lane = g * 128 + j * chans
                for s in range(2):
                    ms[p, pl.ds((nl * 2 + s) * kc + q * 4 + j, gx, stride=xblk), :] = jnp.concatenate(
                        [back[(x * 2 + s) * gx : (x * 2 + s + 1) * gx, lane : lane + chans] for x in range(rx)], axis=1)
        each(xcopy, start, gx, *margs, p)
        keep_own(ms, mr, p, mx, xblk)

    halo(2).wait_recv()
    halo(3).wait_recv()
    lax.fori_loop(ry // 2, ry, local_part, 0)
    local_part(0, 0)

    for p in range(pieces):
        each(xarrived, got, gx, *margs, p)
        data = jnp.concatenate([mr[p, pl.ds(k, 2 * modes, stride=kc), :] for k in range(kc)], axis=1)
        tall = dot(yback[...], data)
        for k in range(kc):
            ts[p, pl.ds(k, 2 * full_y, stride=kc), :] = tall[:, k * lanes : (k + 1) * lanes]
        each(ycopy, start, gy, *targs, p)
        keep_own(ts, tr, p, my, yblk)
    for p in range(pieces):
        each(yarrived, got, gy, *targs, p)

    def finish(y, carry):
        rows = [tr[p, pl.ds(pl.multiple_of((g * ry + y) * 2 * kc, 8), 2 * kc), :]
                for p in range(pieces) for g in range(gy)]
        spectral = dot(jnp.concatenate(rows, axis=0), zback[...], ((0,), (0,)))
        v = spectral.reshape(rx, chans, depth) + out[y]
        inner = np.float32(np.sqrt(2.0 / np.pi)) * (v + np.float32(0.044715) * (v * v * v))
        out[y] = 0.5 * v * (1.0 + jnp.tanh(inner))
        return carry

    lax.fori_loop(0, ry, finish, 0)

    for i in range(4):
        halo(i).wait_send()
    for p in range(pieces):
        each(ycopy, sent, gy, *zargs, p)
        each(xcopy, sent, gx, *yargs, p)
        each(xcopy, sent, gx, *margs, p)
        each(ycopy, sent, gy, *targs, p)


def on_device(field, spec_weight, dw_kernel, point_weight, bias):
    gx, gy = lax.axis_size("gx"), lax.axis_size("gy")
    chans, rx, ry, depth = field.shape
    modes, nlc, kl = spec_weight.shape[1:4]
    lanes = rx * chans
    f32 = jnp.float32
    pieces = 2 if kl % 8 == 0 else 1
    kc = kl // pieces
    cfg = (gx, gy, rx, ry, depth, modes, pieces)

    cells = jnp.transpose(field, (2, 1, 0, 3))
    taps = jnp.broadcast_to(dw_kernel.reshape(chans, 27).T[:, :, None], (27, chans, 128))
    point = jnp.kron(jnp.eye(rx, dtype=f32), point_weight.T)
    biases = jnp.broadcast_to(bias[:, None], (chans, 128))
    vmem = pl.BlockSpec(memory_space=pltpu.VMEM)
    ybuf = pltpu.VMEM((pieces, gy * ry * 2 * kc, lanes), f32)
    xbuf = pltpu.VMEM((pieces, gx * nlc * 2 * kc, lanes), f32)
    dma = pltpu.SemaphoreType.DMA
    out = pl.pallas_call(
        functools.partial(layer_kernel, cfg),
        in_specs=[vmem] * 10 + [pl.BlockSpec(memory_space=pl.ANY)],
        out_specs=vmem,
        out_shape=jax.ShapeDtypeStruct((ry, rx, chans, depth), f32),
        scratch_shapes=[
            pltpu.VMEM(spec_weight.shape, f32),
            pltpu.VMEM((ry + 2, rx + 2, chans, depth), f32),
            ybuf, ybuf, xbuf, xbuf, xbuf, xbuf, ybuf, ybuf,
            pltpu.VMEM((nlc * kc // 4 * chans, 8 * modes), f32),
            pltpu.VMEM((nlc * kc // 4, 16 * modes, 128), f32),
            dma((pieces,)),
            dma((pieces, gy)), dma((pieces, gy)), dma((pieces, gx)), dma((pieces, gx)),
            dma((pieces, gx)), dma((pieces, gx)), dma((pieces, gy)), dma((pieces, gy)),
            dma((4,)), dma((4,)),
        ],
        compiler_params=params(60, collective_id=0, has_side_effects=True),
        name="layer",
    )(*tables(cfg), taps, point, biases, cells, spec_weight)
    return jnp.transpose(out, (2, 1, 0, 3))


def solution(mesh):
    placed = (P(None, "gx", "gy", None), P(None, None, "gx", "gy", None, None), P(), P(), P())
    return jax.shard_map(
        on_device, mesh=mesh, in_specs=placed, out_specs=P(None, "gx", "gy", None), check_vma=False
    )
```

```python
import functools

import jax
import jax.numpy as jnp
import ml_dtypes
import numpy as np
from jax import lax
from jax.experimental import pallas as pl
from jax.experimental.pallas import tpu as pltpu
from jax.sharding import PartitionSpec as P

MIB = 1 << 20


def params(mib, **more):
    return pltpu.CompilerParams(vmem_limit_bytes=mib * MIB, **more)


def halves(a):
    high = a.astype(jnp.bfloat16)
    return high, (a - high.astype(jnp.float32)).astype(jnp.bfloat16)


def left(a, axis):
    high, low = halves(a)
    return jnp.concatenate([high, low, high], axis=axis)


def right(a, axis):
    high, low = halves(a)
    return jnp.concatenate([high, high, low], axis=axis)


def table_halves(a):
    high = a.astype(ml_dtypes.bfloat16)
    return high, (a - high.astype(np.float32)).astype(ml_dtypes.bfloat16)


def table_left(a):
    high, low = table_halves(a)
    return np.concatenate([high, low, high], axis=1)


def table_right(a):
    high, low = table_halves(a)
    return np.concatenate([high, high, low], axis=0)


def dot(a, b, dims=((1,), (0,))):
    return lax.dot_general(a, b, (dims, ((), ())), preferred_element_type=jnp.float32)


def kept(modes, length):
    index = np.arange(modes)
    return np.where(index < modes // 2, index, index + length - modes)


def waves(freqs, length):
    angle = (freqs[:, None] * np.arange(length)[None, :] % length) * (2.0 * np.pi / length)
    return np.cos(angle), np.sin(angle)


def table_pair(modes, length, direction):
    cosine, sine = waves(kept(modes, length), length)
    upper = np.stack([cosine, direction * sine])
    lower = np.stack([-direction * sine, cosine])
    return np.stack([upper, lower])


def rows_z(modes, depth, groups, pieces, table):
    kc = modes // (groups * pieces)
    return table.reshape(2, groups, pieces, kc, depth).transpose(2, 1, 0, 3, 4).reshape(2 * modes, depth).astype(np.float32)


def tables(cfg):
    gx, gy, rx, ry, depth, modes, pieces = cfg
    full_x, full_y = rx * gx, ry * gy
    cosine, sine = waves(np.arange(modes), depth)
    zfwd = rows_z(modes, depth, gy, pieces, np.stack([cosine, -sine]))
    weight = (np.where(np.arange(modes) == 0, 1.0, 2.0) / depth)[:, None]
    zback = rows_z(modes, depth, gy, pieces, np.stack([weight * cosine, -weight * sine]))
    yfwd = table_pair(modes, full_y, 1.0).transpose(2, 0, 1, 3).reshape(2 * modes, 2 * full_y).astype(np.float32)
    yback = (table_pair(modes, full_y, -1.0) / full_y).transpose(3, 0, 2, 1)
    yback = yback.reshape(2 * full_y, 2 * modes).astype(np.float32)
    xtab = table_pair(modes, full_x, 1.0).reshape(2, 2, modes, gx, rx).transpose(4, 1, 3, 0, 2)
    xfwd = np.zeros((rx, 4, 2, gx, 4, 2, modes), np.float32)
    for j in range(4):
        xfwd[:, j, :, :, j] = xtab
    xfwd = xfwd.reshape(rx * 8 * gx, 8 * modes)
    xback = (table_pair(modes, full_x, -1.0) / full_x).reshape(2, 2, modes, gx, rx)
    xback = xback.transpose(4, 0, 3, 1, 2).reshape(rx * 2 * gx, 2 * modes)
    xback = np.repeat(xback, 8, axis=1).astype(np.float32)
    return (table_left(zfwd), table_left(yfwd), table_right(xfwd), table_left(xback), table_left(yback),
            table_right(zback))


def layer_kernel(cfg, zfwd, yfwd, xfwd, xback, yback, zback, dw, pw, bias, field_hbm, weight_hbm, out_hbm,
                 weight, pad, raw, acc, taps, small, point, zs, zr, ys, yr, ms, mr, ts, tr, spec, parts,
                 fsem, wsem, zss, zrs, yss, yrs, mss, mrs, tss, trs, hss, hrs):
    gx, gy, rx, ry, depth, modes, pieces = cfg
    chans = pad.shape[2]
    lanes = rx * chans
    full_y = ry * gy
    nlc, kl = weight.shape[2:4]
    kc = kl // pieces
    quads = kc // 4
    groups = nlc * quads
    xblk = nlc * 2 * kc
    yblk = ry * 2 * kc
    mx, my = lax.axis_index("gx"), lax.axis_index("gy")
    MESH = pl.DeviceIdType.MESH

    def weight_copy(p):
        at = pl.ds(p * kc, kc)
        return pltpu.make_async_copy(weight_hbm.at[:, :, :, at], weight.at[:, :, :, at], wsem.at[p])

    tiles = [(h, x) for x in range(rx) for h in range(depth // 128)]

    def field_copy(i):
        h, x = tiles[i]
        return pltpu.make_async_copy(field_hbm.at[:, x, :, pl.ds(h * 128, 128)], raw.at[h, x], fsem.at[i])

    for i in range(len(tiles)):
        field_copy(i).start()
    for p in range(pieces):
        weight_copy(p).start()

    barrier = pltpu.get_barrier_semaphore()
    for d in range(1, gx):
        pl.semaphore_signal(barrier, inc=1, device_id=(lax.rem(mx + d, gx), my), device_id_type=MESH)
    for d in range(1, gy):
        pl.semaphore_signal(barrier, inc=1, device_id=(mx, lax.rem(my + d, gy)), device_id_type=MESH)

    def block(ref, p, at, rows):
        return ref.at[p, pl.ds(pl.multiple_of(at * rows, 8), rows)]

    def xcopy(src, dst, ssem, rsem, p, d):
        to = lax.rem(mx + d, gx)
        return pltpu.make_async_remote_copy(
            src_ref=block(src, p, to, xblk), dst_ref=block(dst, p, mx, xblk), send_sem=ssem.at[p, to],
            recv_sem=rsem.at[p, mx], device_id=(to, my), device_id_type=MESH)

    def xarrived(src, dst, ssem, rsem, p, d):
        of = lax.rem(mx + d, gx)
        return pltpu.make_async_remote_copy(
            src_ref=block(src, p, of, xblk), dst_ref=block(dst, p, of, xblk), send_sem=ssem.at[p, of],
            recv_sem=rsem.at[p, of], device_id=(of, my), device_id_type=MESH)

    def ycopy(src, dst, ssem, rsem, p, d):
        to = lax.rem(my + d, gy)
        return pltpu.make_async_remote_copy(
            src_ref=block(src, p, to, yblk), dst_ref=block(dst, p, my, yblk), send_sem=ssem.at[p, to],
            recv_sem=rsem.at[p, my], device_id=(mx, to), device_id_type=MESH)

    def yarrived(src, dst, ssem, rsem, p, d):
        of = lax.rem(my + d, gy)
        return pltpu.make_async_remote_copy(
            src_ref=block(src, p, of, yblk), dst_ref=block(dst, p, of, yblk), send_sem=ssem.at[p, of],
            recv_sem=rsem.at[p, of], device_id=(mx, of), device_id_type=MESH)

    def each(make, act, count, *args):
        def step(d, carry):
            act(make(*args, d))
            return carry
        lax.fori_loop(1, count, step, 0)

    start, sent, got = lambda c: c.start(), lambda c: c.wait_send(), lambda c: c.wait_recv()
    zargs, yargs = (zs, zr, zss, zrs), (ys, yr, yss, yrs)
    margs, targs = (ms, mr, mss, mrs), (ts, tr, tss, trs)

    def keep_own(src, dst, p, at, rows):
        own = pl.ds(pl.multiple_of(at * rows, 8), rows)
        dst[p, own, :] = src[p, own, :]

    def halo(i):
        if i < 2:
            to = lax.rem(mx + (1 if i == 0 else gx - 1), gx)
            src = pad.at[pl.ds(1, ry), pl.ds(rx if i == 0 else 1, 1)]
            dst = pad.at[pl.ds(1, ry), pl.ds(0 if i == 0 else rx + 1, 1)]
            where = (to, my)
        else:
            to = lax.rem(my + (1 if i == 2 else gy - 1), gy)
            src = pad.at[pl.ds(ry if i == 2 else 1, 1)]
            dst = pad.at[pl.ds(0 if i == 2 else ry + 1, 1)]
            where = (mx, to)
        return pltpu.make_async_remote_copy(
            src_ref=src, dst_ref=dst, send_sem=hss.at[i], recv_sem=hrs.at[i], device_id=where, device_id_type=MESH)

    small[...] = jnp.zeros_like(small)
    for i in range(9):
        small[3 * i : 3 * i + 3, :chans] = dw[i // 3, i % 3]
    small[27:28, :chans] = bias[...]
    turned_small = small[...].T
    for i in range(28):
        taps[i] = jnp.broadcast_to(turned_small[:chans, i : i + 1], (chans, 128))
    small[...] = jnp.zeros_like(small)
    for x in range(rx):
        small[x * chans : (x + 1) * chans, x * chans : (x + 1) * chans] = pw[...]
    point[...] = left(small[...].T, 1)

    for i in range(len(tiles)):
        field_copy(i).wait()
    flat = raw.reshape(depth // 128, rx, chans * ry, 128)

    def forward(i, carry):
        data = []
        for yy in range(4):
            y = i * 4 + yy
            for x in range(rx):
                cell = jnp.concatenate(
                    [flat[h, x, pl.ds(y, chans, stride=ry), :] for h in range(depth // 128)], axis=1)
                pad[y + 1, x + 1] = cell
                data.append(cell)
        zspec = dot(zfwd[...], right(jnp.concatenate(data, axis=0), 1), ((1,), (1,)))
        for yy in range(4):
            for p in range(pieces):
                for g in range(gy):
                    at = (p * gy + g) * 2 * kc
                    row = pl.ds(pl.multiple_of((g * ry + i * 4 + yy) * 2 * kc, 8), 2 * kc)
                    zs[p, row, :] = zspec[at : at + 2 * kc, yy * lanes : (yy + 1) * lanes]
        return carry

    lax.fori_loop(0, ry // 4, forward, 0)

    pl.semaphore_wait(barrier, gx + gy - 2)
    for p in range(pieces):
        each(ycopy, start, gy, *zargs, p)
    halo(0).start()
    halo(1).start()

    def second(p, carry):
        keep_own(zs, zr, p, my, yblk)
        each(yarrived, got, gy, *zargs, p)
        data = jnp.concatenate([
            jnp.concatenate([zr[p, pl.ds(r * kc + k, full_y, stride=2 * kc), :] for r in range(2)], axis=0)
            for k in range(kc)], axis=1)
        yspec = dot(yfwd[...], right(data, 0))
        for k in range(kc):
            ys[p, pl.ds(k, 2 * modes, stride=kc), :] = yspec[:, k * lanes : (k + 1) * lanes]
        each(xcopy, start, gx, *yargs, p)
        keep_own(ys, yr, p, mx, xblk)
        return carry

    lax.fori_loop(0, pieces, second, 0)

    halo(0).wait_recv()
    halo(1).wait_recv()
    halo(2).start()
    halo(3).start()

    def local_part(y, carry):
        here = pad[y + 1, pl.ds(1, rx)].reshape(lanes, depth)
        base = dot(point[...], right(here, 0))
        for cc in range(0, chans, 8):
            sums = [[None] * 3 for _ in range(rx)]
            for b in range(3):
                for xp in range(rx + 2):
                    value = pad[y + b, xp, cc : cc + 8, :]
                    for a in range(3):
                        x = xp - a
                        if 0 <= x < rx:
                            for e in range(3):
                                tap = taps[(a * 3 + b) * 3 + e, cc : cc + 8, :]
                                term = jnp.concatenate([tap] * (depth // 128), axis=1) * value
                                sums[x][e] = term if sums[x][e] is None else sums[x][e] + term
            shift = jnp.concatenate([taps[27, cc : cc + 8, :]] * (depth // 128), axis=1)
            for x in range(rx):
                total = sums[x][1] + pltpu.roll(sums[x][0], 1, 1) + pltpu.roll(sums[x][2], depth - 1, 1)
                acc[y, x, cc : cc + 8, :] = total + base[x * chans + cc : x * chans + cc + 8, :] + shift
        return carry

    lax.fori_loop(1, ry // 2, local_part, 0)

    def channels(p, before):
        each(xarrived, got, gx, *yargs, p)
        gathered = []
        for g in range(groups):
            nl, q = g // quads, g % quads
            data = jnp.concatenate(
                [yr[p, pl.ds((nl * 2 + s) * kc + q * 4 + j, gx, stride=xblk), :] for j in range(4) for s in range(2)],
                axis=0)
            turned = data.T
            gathered.append(jnp.concatenate([turned[x * chans : (x + 1) * chans] for x in range(rx)], axis=1))
        spec[...] = dot(left(jnp.concatenate(gathered, axis=0), 1), xfwd[...])
        weight_copy(p).wait()

        def mix(g, carry):
            nl, q = g // quads, g % quads
            at = pl.ds(pl.multiple_of(g * chans, 8), chans)
            for m in range(modes):
                res, ims = [], []
                for j in range(4):
                    lane = j * 2 * modes + m
                    half = spec[at, j * 2 * modes // 128 * 128 : j * 2 * modes // 128 * 128 + 128]
                    lane = lane % 128
                    re = jnp.broadcast_to(half[:, lane : lane + 1], (chans, chans))
                    im = jnp.broadcast_to(half[:, lane + modes : lane + modes + 1], (chans, chans))
                    wre = weight[0, m, nl, p * kc + q * 4 + j]
                    wim = weight[1, m, nl, p * kc + q * 4 + j]
                    mre = re * wre - im * wim
                    mim = re * wim + im * wre
                    res.append(sum(mre[i : i + 8] for i in range(8, chans, 8)) + mre[:8])
                    ims.append(sum(mim[i : i + 8] for i in range(8, chans, 8)) + mim[:8])
                parts[g, m * 8 : m * 8 + 8, :] = jnp.concatenate(res, axis=1)
                parts[g, (modes + m) * 8 : (modes + m) * 8 + 8, :] = jnp.concatenate(ims, axis=1)
            return carry

        lax.fori_loop(0, groups, mix, 0)
        back = dot(xback[...], right(jnp.concatenate([parts[g] for g in range(groups)], axis=1), 0))
        for g in range(groups):
            nl, q = g // quads, g % quads
            for j in range(4):
                lane = g * 128 + j * chans
                for s in range(2):
                    ms[p, pl.ds((nl * 2 + s) * kc + q * 4 + j, gx, stride=xblk), :] = jnp.concatenate(
                        [back[(x * 2 + s) * gx : (x * 2 + s + 1) * gx, lane : lane + chans] for x in range(rx)], axis=1)
        each(xcopy, start, gx, *margs, p)
        keep_own(ms, mr, p, mx, xblk)
        return before

    lax.fori_loop(0, pieces, channels, 0)

    halo(2).wait_recv()
    halo(3).wait_recv()
    lax.fori_loop(ry // 2, ry + 1, lambda y, carry: local_part(lax.rem(y, ry), carry), 0)

    def second_back(p, carry):
        each(xarrived, got, gx, *margs, p)
        data = jnp.concatenate([mr[p, pl.ds(k, 2 * modes, stride=kc), :] for k in range(kc)], axis=1)
        tall = dot(yback[...], right(data, 0))
        for k in range(kc):
            ts[p, pl.ds(k, 2 * full_y, stride=kc), :] = tall[:, k * lanes : (k + 1) * lanes]
        each(ycopy, start, gy, *targs, p)
        keep_own(ts, tr, p, my, yblk)
        return carry

    lax.fori_loop(0, pieces, second_back, 0)
    for p in range(pieces):
        each(yarrived, got, gy, *targs, p)

    def finish(i, carry):
        data = jnp.concatenate([
            jnp.concatenate([
                tr[p, pl.ds(pl.multiple_of((g * ry + i * 4 + yy) * 2 * kc, 8), 2 * kc), :]
                for p in range(pieces) for g in range(gy)], axis=0)
            for yy in range(4)], axis=1)
        spectral = dot(left(data, 0), zback[...], ((0,), (0,)))
        for yy in range(4):
            y = i * 4 + yy
            for x in range(rx):
                at = yy * lanes + x * chans
                total = spectral[at : at + chans] + acc[y, x]
                for h in range(depth // 128):
                    flat[h, x, pl.ds(y, chans, stride=ry), :] = total[:, h * 128 : (h + 1) * 128]
        return carry

    lax.fori_loop(0, ry // 4, finish, 0)

    def out_copy(i):
        h, x = tiles[i]
        return pltpu.make_async_copy(raw.at[h, x], out_hbm.at[:, x, :, pl.ds(h * 128, 128)], fsem.at[i])

    for i in range(len(tiles)):
        out_copy(i).start()
    for i in range(4):
        halo(i).wait_send()
    for p in range(pieces):
        each(ycopy, sent, gy, *zargs, p)
        each(xcopy, sent, gx, *yargs, p)
        each(xcopy, sent, gx, *margs, p)
        each(ycopy, sent, gy, *targs, p)
    for i in range(len(tiles)):
        out_copy(i).wait()


def on_device(field, spec_weight, dw_kernel, point_weight, bias):
    gx, gy = lax.axis_size("gx"), lax.axis_size("gy")
    chans, rx, ry, depth = field.shape
    modes, nlc, kl = spec_weight.shape[1:4]
    lanes = rx * chans
    f32 = jnp.float32
    pieces = 2 if kl % 8 == 0 else 1
    kc = kl // pieces
    cfg = (gx, gy, rx, ry, depth, modes, pieces)

    vmem = pl.BlockSpec(memory_space=pltpu.VMEM)
    hbm = pl.BlockSpec(memory_space=pl.ANY)
    ybuf = pltpu.VMEM((pieces, gy * ry * 2 * kc, lanes), f32)
    xbuf = pltpu.VMEM((pieces, gx * nlc * 2 * kc, lanes), f32)
    dma = pltpu.SemaphoreType.DMA
    out = pl.pallas_call(
        functools.partial(layer_kernel, cfg),
        in_specs=[vmem] * 9 + [hbm] * 2,
        out_specs=hbm,
        out_shape=jax.ShapeDtypeStruct(field.shape, f32),
        scratch_shapes=[
            pltpu.VMEM(spec_weight.shape, f32),
            pltpu.VMEM((ry + 2, rx + 2, chans, depth), f32),
            pltpu.VMEM((depth // 128, rx, chans, ry, 128), f32),
            pltpu.VMEM((ry, rx, chans, depth), f32),
            pltpu.VMEM((28, chans, 128), f32),
            pltpu.VMEM((lanes, lanes), f32),
            pltpu.VMEM((lanes, 3 * lanes), jnp.bfloat16),
            ybuf, ybuf, xbuf, xbuf, xbuf, xbuf, ybuf, ybuf,
            pltpu.VMEM((nlc * kc // 4 * chans, 8 * modes), f32),
            pltpu.VMEM((nlc * kc // 4, 16 * modes, 128), f32),
            dma((rx * depth // 128,)), dma((pieces,)),
            dma((pieces, gy)), dma((pieces, gy)), dma((pieces, gx)), dma((pieces, gx)),
            dma((pieces, gx)), dma((pieces, gx)), dma((pieces, gy)), dma((pieces, gy)),
            dma((4,)), dma((4,)),
        ],
        compiler_params=params(60, collective_id=0, has_side_effects=True),
        name="layer",
    )(*tables(cfg), jnp.transpose(dw_kernel, (1, 2, 3, 0)), point_weight, bias[None], field, spec_weight)
    return jax.nn.gelu(out)


def solution(mesh):
    placed = (P(None, "gx", "gy", None), P(None, None, "gx", "gy", None, None), P(), P(), P())
    return jax.shard_map(
        on_device, mesh=mesh, in_specs=placed, out_specs=P(None, "gx", "gy", None), check_vma=False
    )
```

```python
import functools

import jax
import jax.numpy as jnp
import ml_dtypes
import numpy as np
from jax import lax
from jax.experimental import pallas as pl
from jax.experimental.pallas import tpu as pltpu
from jax.sharding import PartitionSpec as P

MIB = 1 << 20


def params(mib, **more):
    return pltpu.CompilerParams(vmem_limit_bytes=mib * MIB, **more)


def halves(a):
    high = a.astype(jnp.bfloat16)
    return high, (a - high.astype(jnp.float32)).astype(jnp.bfloat16)


def left(a, axis):
    high, low = halves(a)
    return jnp.concatenate([high, low, high], axis=axis)


def right(a, axis):
    high, low = halves(a)
    return jnp.concatenate([high, high, low], axis=axis)


def table_halves(a):
    high = a.astype(ml_dtypes.bfloat16)
    return high, (a - high.astype(np.float32)).astype(ml_dtypes.bfloat16)


def table_left(a):
    high, low = table_halves(a)
    return np.concatenate([high, low, high], axis=1)


def table_right(a):
    high, low = table_halves(a)
    return np.concatenate([high, high, low], axis=0)


def dot(a, b, dims=((1,), (0,))):
    return lax.dot_general(a, b, (dims, ((), ())), preferred_element_type=jnp.float32)


def kept(modes, length):
    index = np.arange(modes)
    return np.where(index < modes // 2, index, index + length - modes)


def waves(freqs, length):
    angle = (freqs[:, None] * np.arange(length)[None, :] % length) * (2.0 * np.pi / length)
    return np.cos(angle), np.sin(angle)


def table_pair(modes, length, direction):
    cosine, sine = waves(kept(modes, length), length)
    upper = np.stack([cosine, direction * sine])
    lower = np.stack([-direction * sine, cosine])
    return np.stack([upper, lower])


def rows_z(modes, depth, groups, pieces, table):
    kc = modes // (groups * pieces)
    return table.reshape(2, groups, pieces, kc, depth).transpose(2, 1, 0, 3, 4).reshape(2 * modes, depth).astype(np.float32)


def tables(cfg):
    gx, gy, rx, ry, depth, modes, pieces = cfg
    full_x, full_y = rx * gx, ry * gy
    cosine, sine = waves(np.arange(modes), depth)
    zfwd = rows_z(modes, depth, gy, pieces, np.stack([cosine, -sine]))
    weight = (np.where(np.arange(modes) == 0, 1.0, 2.0) / depth)[:, None]
    zback = rows_z(modes, depth, gy, pieces, np.stack([weight * cosine, -weight * sine]))
    yfwd = table_pair(modes, full_y, 1.0).transpose(2, 0, 1, 3).reshape(2 * modes, 2 * full_y).astype(np.float32)
    yback = (table_pair(modes, full_y, -1.0) / full_y).transpose(3, 0, 2, 1)
    yback = yback.reshape(2 * full_y, 2 * modes).astype(np.float32)
    xtab = table_pair(modes, full_x, 1.0).reshape(2, 2, modes, gx, rx).transpose(4, 1, 3, 0, 2)
    xfwd = np.zeros((rx, 4, 2, gx, 4, 2, modes), np.float32)
    for j in range(4):
        xfwd[:, j, :, :, j] = xtab
    xfwd = xfwd.reshape(rx * 8 * gx, 8 * modes)
    xback = (table_pair(modes, full_x, -1.0) / full_x).reshape(2, 2, modes, gx, rx)
    xback = xback.transpose(4, 0, 3, 1, 2).reshape(rx * 2 * gx, 2 * modes)
    xback = np.repeat(xback, 8, axis=1).astype(np.float32)
    return (table_left(zfwd), table_left(yfwd), table_right(xfwd), table_left(xback), table_left(yback),
            table_right(zback))


def layer_kernel(cfg, zfwd, yfwd, xfwd, xback, yback, zback, dw, pw, bias, field_hbm, weight_hbm, out_hbm,
                 weight, pad, raw, acc, taps, small, point, zs, zr, ys, yr, ms, mr, ts, tr, spec, parts,
                 fsem, wsem, zss, zrs, yss, yrs, mss, mrs, tss, trs, hss, hrs):
    gx, gy, rx, ry, depth, modes, pieces = cfg
    chans = pad.shape[2]
    lanes = rx * chans
    full_y = ry * gy
    nlc, kl = weight.shape[2:4]
    kc = kl // pieces
    quads = kc // 4
    groups = nlc * quads
    xblk = nlc * 2 * kc
    yblk = ry * 2 * kc
    mx, my = lax.axis_index("gx"), lax.axis_index("gy")
    MESH = pl.DeviceIdType.MESH

    def weight_copy(p):
        at = pl.ds(p * kc, kc)
        return pltpu.make_async_copy(weight_hbm.at[:, :, :, at], weight.at[:, :, :, at], wsem.at[p])

    tiles = [(h, x) for x in range(rx) for h in range(depth // 128)]

    def field_copy(i):
        h, x = tiles[i]
        return pltpu.make_async_copy(field_hbm.at[:, x, :, pl.ds(h * 128, 128)], raw.at[h, x], fsem.at[i])

    for i in range(len(tiles)):
        field_copy(i).start()
    for p in range(pieces):
        weight_copy(p).start()

    barrier = pltpu.get_barrier_semaphore()
    for d in range(1, gx):
        pl.semaphore_signal(barrier, inc=1, device_id=(lax.rem(mx + d, gx), my), device_id_type=MESH)
    for d in range(1, gy):
        pl.semaphore_signal(barrier, inc=1, device_id=(mx, lax.rem(my + d, gy)), device_id_type=MESH)

    def block(ref, p, at, rows):
        return ref.at[p, pl.ds(pl.multiple_of(at * rows, 8), rows)]

    def xcopy(src, dst, ssem, rsem, p, i):
        half = (i + 1) // 2
        to = lax.rem(mx + gx // 2 + half * (1 - 2 * lax.rem(i, 2)) + gx, gx)
        return pltpu.make_async_remote_copy(
            src_ref=block(src, p, to, xblk), dst_ref=block(dst, p, mx, xblk), send_sem=ssem.at[p],
            recv_sem=rsem.at[p], device_id=(to, my), device_id_type=MESH)

    def ycopy(src, dst, ssem, rsem, p, d):
        to = lax.rem(my + d + 1, gy)
        return pltpu.make_async_remote_copy(
            src_ref=block(src, p, to, yblk), dst_ref=block(dst, p, my, yblk), send_sem=ssem.at[p],
            recv_sem=rsem.at[p], device_id=(mx, to), device_id_type=MESH)

    def xall(src, dst, ssem, rsem, p):
        rows = pl.ds(0, (gx - 1) * xblk)
        return pltpu.make_async_remote_copy(
            src_ref=src.at[p, rows], dst_ref=dst.at[p, rows], send_sem=ssem.at[p], recv_sem=rsem.at[p],
            device_id=(lax.rem(mx + 1, gx), my), device_id_type=MESH)

    def yall(src, dst, ssem, rsem, p):
        rows = pl.ds(0, (gy - 1) * yblk)
        return pltpu.make_async_remote_copy(
            src_ref=src.at[p, rows], dst_ref=dst.at[p, rows], send_sem=ssem.at[p], recv_sem=rsem.at[p],
            device_id=(mx, lax.rem(my + 1, gy)), device_id_type=MESH)

    def each(make, count, *args):
        def step(i, carry):
            make(*args, i).start()
            return carry
        lax.fori_loop(0, count - 1, step, 0)

    zargs, yargs = (zs, zr, zss, zrs), (ys, yr, yss, yrs)
    margs, targs = (ms, mr, mss, mrs), (ts, tr, tss, trs)

    def keep_own(src, dst, p, at, rows):
        own = pl.ds(pl.multiple_of(at * rows, 8), rows)
        dst[p, own, :] = src[p, own, :]

    def halo(i):
        if i < 2:
            to = lax.rem(mx + (1 if i == 0 else gx - 1), gx)
            src = pad.at[pl.ds(1, ry), pl.ds(rx if i == 0 else 1, 1)]
            dst = pad.at[pl.ds(1, ry), pl.ds(0 if i == 0 else rx + 1, 1)]
            where = (to, my)
        else:
            to = lax.rem(my + (1 if i == 2 else gy - 1), gy)
            src = pad.at[pl.ds(ry if i == 2 else 1, 1)]
            dst = pad.at[pl.ds(0 if i == 2 else ry + 1, 1)]
            where = (mx, to)
        return pltpu.make_async_remote_copy(
            src_ref=src, dst_ref=dst, send_sem=hss.at[i], recv_sem=hrs.at[i], device_id=where, device_id_type=MESH)

    small[...] = jnp.zeros_like(small)
    for i in range(9):
        small[3 * i : 3 * i + 3, :chans] = dw[i // 3, i % 3]
    small[27:28, :chans] = bias[...]
    turned_small = small[...].T
    for i in range(28):
        taps[i] = jnp.broadcast_to(turned_small[:chans, i : i + 1], (chans, 128))
    small[...] = jnp.zeros_like(small)
    for x in range(rx):
        small[x * chans : (x + 1) * chans, x * chans : (x + 1) * chans] = pw[...]
    point[...] = left(small[...].T, 1)

    for i in range(len(tiles)):
        field_copy(i).wait()
    flat = raw.reshape(depth // 128, rx, chans * ry, 128)

    def forward(i, carry):
        data = []
        for yy in range(4):
            y = i * 4 + yy
            for x in range(rx):
                cell = jnp.concatenate(
                    [flat[h, x, pl.ds(y, chans, stride=ry), :] for h in range(depth // 128)], axis=1)
                pad[y + 1, x + 1] = cell
                data.append(cell)
        zspec = dot(zfwd[...], right(jnp.concatenate(data, axis=0), 1), ((1,), (1,)))
        for yy in range(4):
            for p in range(pieces):
                for g in range(gy):
                    at = (p * gy + g) * 2 * kc
                    row = pl.ds(pl.multiple_of((g * ry + i * 4 + yy) * 2 * kc, 8), 2 * kc)
                    zs[p, row, :] = zspec[at : at + 2 * kc, yy * lanes : (yy + 1) * lanes]
        return carry

    lax.fori_loop(0, ry // 4, forward, 0)

    pl.semaphore_wait(barrier, gx + gy - 2)
    for p in range(pieces):
        each(ycopy, gy, *zargs, p)

    def second(p, carry):
        keep_own(zs, zr, p, my, yblk)
        yall(*zargs, p).wait_recv()
        data = jnp.concatenate([
            jnp.concatenate([zr[p, pl.ds(r * kc + k, full_y, stride=2 * kc), :] for r in range(2)], axis=0)
            for k in range(kc)], axis=1)
        yspec = dot(yfwd[...], right(data, 0))
        for k in range(kc):
            ys[p, pl.ds(k, 2 * modes, stride=kc), :] = yspec[:, k * lanes : (k + 1) * lanes]
        each(xcopy, gx, *yargs, p)
        keep_own(ys, yr, p, mx, xblk)
        return carry

    lax.fori_loop(0, pieces, second, 0)

    def local_part(y, carry):
        here = pad[y + 1, pl.ds(1, rx)].reshape(lanes, depth)
        base = dot(point[...], right(here, 0))
        for cc in range(0, chans, 8):
            sums = [[None] * 3 for _ in range(rx)]
            for b in range(3):
                for xp in range(rx + 2):
                    value = pad[y + b, xp, cc : cc + 8, :]
                    for a in range(3):
                        x = xp - a
                        if 0 <= x < rx:
                            for e in range(3):
                                tap = taps[(a * 3 + b) * 3 + e, cc : cc + 8, :]
                                term = jnp.concatenate([tap] * (depth // 128), axis=1) * value
                                sums[x][e] = term if sums[x][e] is None else sums[x][e] + term
            shift = jnp.concatenate([taps[27, cc : cc + 8, :]] * (depth // 128), axis=1)
            for x in range(rx):
                total = sums[x][1] + pltpu.roll(sums[x][0], 1, 1) + pltpu.roll(sums[x][2], depth - 1, 1)
                acc[y, x, cc : cc + 8, :] = total + base[x * chans + cc : x * chans + cc + 8, :] + shift
        return carry

    def channels(p, before):
        xall(*yargs, p).wait_recv()

        @pl.when(p == 0)
        def _():
            halo(0).start()
            halo(1).start()

        gathered = []
        for g in range(groups):
            nl, q = g // quads, g % quads
            data = jnp.concatenate(
                [yr[p, pl.ds((nl * 2 + s) * kc + q * 4 + j, gx, stride=xblk), :] for j in range(4) for s in range(2)],
                axis=0)
            turned = data.T
            gathered.append(jnp.concatenate([turned[x * chans : (x + 1) * chans] for x in range(rx)], axis=1))
        spec[...] = dot(left(jnp.concatenate(gathered, axis=0), 1), xfwd[...])
        weight_copy(p).wait()

        def mix(g, carry):
            nl, q = g // quads, g % quads
            at = pl.ds(pl.multiple_of(g * chans, 8), chans)
            for m in range(modes):
                res, ims = [], []
                for j in range(4):
                    lane = j * 2 * modes + m
                    half = spec[at, j * 2 * modes // 128 * 128 : j * 2 * modes // 128 * 128 + 128]
                    lane = lane % 128
                    re = jnp.broadcast_to(half[:, lane : lane + 1], (chans, chans))
                    im = jnp.broadcast_to(half[:, lane + modes : lane + modes + 1], (chans, chans))
                    wre = weight[0, m, nl, p * kc + q * 4 + j]
                    wim = weight[1, m, nl, p * kc + q * 4 + j]
                    mre = re * wre - im * wim
                    mim = re * wim + im * wre
                    res.append(sum(mre[i : i + 8] for i in range(8, chans, 8)) + mre[:8])
                    ims.append(sum(mim[i : i + 8] for i in range(8, chans, 8)) + mim[:8])
                parts[g, m * 8 : m * 8 + 8, :] = jnp.concatenate(res, axis=1)
                parts[g, (modes + m) * 8 : (modes + m) * 8 + 8, :] = jnp.concatenate(ims, axis=1)
            return carry

        lax.fori_loop(0, groups, mix, 0)
        back = dot(xback[...], right(jnp.concatenate([parts[g] for g in range(groups)], axis=1), 0))
        for g in range(groups):
            nl, q = g // quads, g % quads
            for j in range(4):
                lane = g * 128 + j * chans
                for s in range(2):
                    ms[p, pl.ds((nl * 2 + s) * kc + q * 4 + j, gx, stride=xblk), :] = jnp.concatenate(
                        [back[(x * 2 + s) * gx : (x * 2 + s + 1) * gx, lane : lane + chans] for x in range(rx)], axis=1)
        each(xcopy, gx, *margs, p)
        keep_own(ms, mr, p, mx, xblk)

        @pl.when(p == 0)
        def _():
            halo(0).wait_recv()
            halo(1).wait_recv()
            halo(2).start()
            halo(3).start()

        return before

    lax.fori_loop(0, pieces, channels, 0)

    halo(2).wait_recv()
    halo(3).wait_recv()
    lax.fori_loop(0, ry, local_part, 0)

    def second_back(p, carry):
        xall(*margs, p).wait_recv()
        data = jnp.concatenate([mr[p, pl.ds(k, 2 * modes, stride=kc), :] for k in range(kc)], axis=1)
        tall = dot(yback[...], right(data, 0))
        for k in range(kc):
            ts[p, pl.ds(k, 2 * full_y, stride=kc), :] = tall[:, k * lanes : (k + 1) * lanes]
        each(ycopy, gy, *targs, p)
        keep_own(ts, tr, p, my, yblk)
        return carry

    lax.fori_loop(0, pieces, second_back, 0)
    for p in range(pieces):
        yall(*targs, p).wait_recv()

    def finish(i, carry):
        data = jnp.concatenate([
            jnp.concatenate([
                tr[p, pl.ds(pl.multiple_of((g * ry + i * 4 + yy) * 2 * kc, 8), 2 * kc), :]
                for p in range(pieces) for g in range(gy)], axis=0)
            for yy in range(4)], axis=1)
        spectral = dot(left(data, 0), zback[...], ((0,), (0,)))
        for yy in range(4):
            y = i * 4 + yy
            for x in range(rx):
                at = yy * lanes + x * chans
                total = spectral[at : at + chans] + acc[y, x]
                for h in range(depth // 128):
                    flat[h, x, pl.ds(y, chans, stride=ry), :] = total[:, h * 128 : (h + 1) * 128]
        return carry

    lax.fori_loop(0, ry // 4, finish, 0)

    def out_copy(i):
        h, x = tiles[i]
        return pltpu.make_async_copy(raw.at[h, x], out_hbm.at[:, x, :, pl.ds(h * 128, 128)], fsem.at[i])

    for i in range(len(tiles)):
        out_copy(i).start()
    for i in range(4):
        halo(i).wait_send()
    for p in range(pieces):
        yall(*zargs, p).wait_send()
        xall(*yargs, p).wait_send()
        xall(*margs, p).wait_send()
        yall(*targs, p).wait_send()
    for i in range(len(tiles)):
        out_copy(i).wait()


def on_device(field, spec_weight, dw_kernel, point_weight, bias):
    gx, gy = lax.axis_size("gx"), lax.axis_size("gy")
    chans, rx, ry, depth = field.shape
    modes, nlc, kl = spec_weight.shape[1:4]
    lanes = rx * chans
    f32 = jnp.float32
    pieces = 2 if kl % 8 == 0 else 1
    kc = kl // pieces
    cfg = (gx, gy, rx, ry, depth, modes, pieces)

    vmem = pl.BlockSpec(memory_space=pltpu.VMEM)
    hbm = pl.BlockSpec(memory_space=pl.ANY)
    ybuf = pltpu.VMEM((pieces, gy * ry * 2 * kc, lanes), f32)
    xbuf = pltpu.VMEM((pieces, gx * nlc * 2 * kc, lanes), f32)
    dma = pltpu.SemaphoreType.DMA
    out = pl.pallas_call(
        functools.partial(layer_kernel, cfg),
        in_specs=[vmem] * 9 + [hbm] * 2,
        out_specs=hbm,
        out_shape=jax.ShapeDtypeStruct(field.shape, f32),
        scratch_shapes=[
            pltpu.VMEM(spec_weight.shape, f32),
            pltpu.VMEM((ry + 2, rx + 2, chans, depth), f32),
            pltpu.VMEM((depth // 128, rx, chans, ry, 128), f32),
            pltpu.VMEM((ry, rx, chans, depth), f32),
            pltpu.VMEM((28, chans, 128), f32),
            pltpu.VMEM((lanes, lanes), f32),
            pltpu.VMEM((lanes, 3 * lanes), jnp.bfloat16),
            ybuf, ybuf, xbuf, xbuf, xbuf, xbuf, ybuf, ybuf,
            pltpu.VMEM((nlc * kc // 4 * chans, 8 * modes), f32),
            pltpu.VMEM((nlc * kc // 4, 16 * modes, 128), f32),
            dma((rx * depth // 128,)), dma((pieces,)),
            dma((pieces,)), dma((pieces,)), dma((pieces,)), dma((pieces,)),
            dma((pieces,)), dma((pieces,)), dma((pieces,)), dma((pieces,)),
            dma((4,)), dma((4,)),
        ],
        compiler_params=params(60, collective_id=0, has_side_effects=True),
        name="layer",
    )(*tables(cfg), jnp.transpose(dw_kernel, (1, 2, 3, 0)), point_weight, bias[None], field, spec_weight)
    return jax.nn.gelu(out)


def solution(mesh):
    placed = (P(None, "gx", "gy", None), P(None, None, "gx", "gy", None, None), P(), P(), P())
    return jax.shard_map(
        on_device, mesh=mesh, in_specs=placed, out_specs=P(None, "gx", "gy", None), check_vma=False
    )
```

```python
import functools

import jax
import jax.numpy as jnp
import ml_dtypes
import numpy as np
from jax import lax
from jax.experimental import pallas as pl
from jax.experimental.pallas import tpu as pltpu
from jax.sharding import PartitionSpec as P

MIB = 1 << 20


def params(mib, **more):
    return pltpu.CompilerParams(vmem_limit_bytes=mib * MIB, **more)


def halves(a):
    high = a.astype(jnp.bfloat16)
    return high, (a - high.astype(jnp.float32)).astype(jnp.bfloat16)


def left(a, axis):
    high, low = halves(a)
    return jnp.concatenate([high, low, high], axis=axis)


def right(a, axis):
    high, low = halves(a)
    return jnp.concatenate([high, high, low], axis=axis)


def table_halves(a):
    high = a.astype(ml_dtypes.bfloat16)
    return high, (a - high.astype(np.float32)).astype(ml_dtypes.bfloat16)


def table_left(a):
    high, low = table_halves(a)
    return np.concatenate([high, low, high], axis=1)


def table_right(a):
    high, low = table_halves(a)
    return np.concatenate([high, high, low], axis=0)


def dot(a, b, dims=((1,), (0,))):
    return lax.dot_general(a, b, (dims, ((), ())), preferred_element_type=jnp.float32)


def kept(modes, length):
    index = np.arange(modes)
    return np.where(index < modes // 2, index, index + length - modes)


def waves(freqs, length):
    angle = (freqs[:, None] * np.arange(length)[None, :] % length) * (2.0 * np.pi / length)
    return np.cos(angle), np.sin(angle)


def table_pair(modes, length, direction):
    cosine, sine = waves(kept(modes, length), length)
    upper = np.stack([cosine, direction * sine])
    lower = np.stack([-direction * sine, cosine])
    return np.stack([upper, lower])


def rows_z(modes, depth, groups, pieces, table):
    kc = modes // (groups * pieces)
    return table.reshape(2, groups, pieces, kc, depth).transpose(2, 1, 0, 3, 4).reshape(2 * modes, depth).astype(np.float32)


def tables(cfg):
    gx, gy, rx, ry, depth, modes, pieces = cfg
    full_x, full_y = rx * gx, ry * gy
    cosine, sine = waves(np.arange(modes), depth)
    zfwd = rows_z(modes, depth, gy, pieces, np.stack([cosine, -sine]))
    weight = (np.where(np.arange(modes) == 0, 1.0, 2.0) / depth)[:, None]
    zback = rows_z(modes, depth, gy, pieces, np.stack([weight * cosine, -weight * sine]))
    yfwd = table_pair(modes, full_y, 1.0).transpose(2, 0, 1, 3).reshape(2 * modes, 2 * full_y).astype(np.float32)
    yback = (table_pair(modes, full_y, -1.0) / full_y).transpose(3, 0, 2, 1)
    yback = yback.reshape(2 * full_y, 2 * modes).astype(np.float32)
    xtab = table_pair(modes, full_x, 1.0).reshape(2, 2, modes, gx, rx)
    factor = np.stack([np.stack([xtab[0], xtab[1]]), np.stack([-xtab[1], xtab[0]])])
    xfwd = factor.transpose(0, 3, 1, 5, 2, 4).reshape(4 * modes, rx * 2 * gx)
    xfwd = np.repeat(xfwd, 4, axis=0)
    xtab = (table_pair(modes, full_x, -1.0) / full_x).reshape(2, 2, modes, gx, rx).transpose(4, 0, 3, 2, 1)
    xback = np.zeros((4, rx, 2, gx, modes, 2, 4), np.float32)
    for j in range(4):
        xback[j, ..., j] = xtab
    xback = xback.reshape(4 * rx * 2 * gx, 8 * modes)
    return (table_left(zfwd), table_left(yfwd), table_left(xfwd), table_left(xback), table_left(yback),
            table_right(zback))


def layer_kernel(cfg, zfwd, yfwd, xfwd, xback, yback, zback, dw, pw, bias, field_hbm, weight_hbm, out_hbm,
                 weight, pad, raw, acc, taps, small, point, zs, zr, ys, yr, ms, mr, ts, tr, spec, parts,
                 fsem, wsem, zss, zrs, yss, yrs, mss, mrs, tss, trs, hss, hrs):
    gx, gy, rx, ry, depth, modes, pieces = cfg
    chans = pad.shape[2]
    lanes = rx * chans
    full_y = ry * gy
    nlc, kl = weight.shape[2:4]
    kc = kl // pieces
    quads = kc // 4
    groups = nlc * quads
    xblk = nlc * 2 * kc
    yblk = ry * 2 * kc
    mx, my = lax.axis_index("gx"), lax.axis_index("gy")
    MESH = pl.DeviceIdType.MESH

    def weight_copy(p):
        at = pl.ds(p * kc, kc)
        return pltpu.make_async_copy(weight_hbm.at[:, :, :, at], weight.at[:, :, :, at], wsem.at[p])

    tiles = [(h, x) for x in range(rx) for h in range(depth // 128)]

    def field_copy(i):
        h, x = tiles[i]
        return pltpu.make_async_copy(field_hbm.at[:, x, :, pl.ds(h * 128, 128)], raw.at[h, x], fsem.at[i])

    for i in range(len(tiles)):
        field_copy(i).start()
    for p in range(pieces):
        weight_copy(p).start()

    barrier = pltpu.get_barrier_semaphore()
    for d in range(1, gx):
        pl.semaphore_signal(barrier, inc=1, device_id=(lax.rem(mx + d, gx), my), device_id_type=MESH)
    for d in range(1, gy):
        pl.semaphore_signal(barrier, inc=1, device_id=(mx, lax.rem(my + d, gy)), device_id_type=MESH)

    def block(ref, p, at, rows):
        return ref.at[p, pl.ds(pl.multiple_of(at * rows, 8), rows)]

    def xcopy(src, dst, ssem, rsem, p, i):
        half = (i + 1) // 2
        to = lax.rem(mx + gx // 2 + half * (1 - 2 * lax.rem(i, 2)) + gx, gx)
        return pltpu.make_async_remote_copy(
            src_ref=block(src, p, to, xblk), dst_ref=block(dst, p, mx, xblk), send_sem=ssem.at[p],
            recv_sem=rsem.at[p], device_id=(to, my), device_id_type=MESH)

    def ycopy(src, dst, ssem, rsem, p, d):
        to = lax.rem(my + d + 1, gy)
        return pltpu.make_async_remote_copy(
            src_ref=block(src, p, to, yblk), dst_ref=block(dst, p, my, yblk), send_sem=ssem.at[p],
            recv_sem=rsem.at[p], device_id=(mx, to), device_id_type=MESH)

    def xall(src, dst, ssem, rsem, p):
        rows = pl.ds(0, (gx - 1) * xblk)
        return pltpu.make_async_remote_copy(
            src_ref=src.at[p, rows], dst_ref=dst.at[p, rows], send_sem=ssem.at[p], recv_sem=rsem.at[p],
            device_id=(lax.rem(mx + 1, gx), my), device_id_type=MESH)

    def yall(src, dst, ssem, rsem, p):
        rows = pl.ds(0, (gy - 1) * yblk)
        return pltpu.make_async_remote_copy(
            src_ref=src.at[p, rows], dst_ref=dst.at[p, rows], send_sem=ssem.at[p], recv_sem=rsem.at[p],
            device_id=(mx, lax.rem(my + 1, gy)), device_id_type=MESH)

    def each(make, count, *args):
        def step(i, carry):
            make(*args, i).start()
            return carry
        lax.fori_loop(0, count - 1, step, 0)

    zargs, yargs = (zs, zr, zss, zrs), (ys, yr, yss, yrs)
    margs, targs = (ms, mr, mss, mrs), (ts, tr, tss, trs)

    def keep_own(src, dst, p, at, rows):
        own = pl.ds(pl.multiple_of(at * rows, 8), rows)
        dst[p, own, :] = src[p, own, :]

    def halo(i):
        if i < 2:
            to = lax.rem(mx + (1 if i == 0 else gx - 1), gx)
            src = pad.at[pl.ds(1, ry), pl.ds(rx if i == 0 else 1, 1)]
            dst = pad.at[pl.ds(1, ry), pl.ds(0 if i == 0 else rx + 1, 1)]
            where = (to, my)
        else:
            to = lax.rem(my + (1 if i == 2 else gy - 1), gy)
            src = pad.at[pl.ds(ry if i == 2 else 1, 1)]
            dst = pad.at[pl.ds(0 if i == 2 else ry + 1, 1)]
            where = (mx, to)
        return pltpu.make_async_remote_copy(
            src_ref=src, dst_ref=dst, send_sem=hss.at[i], recv_sem=hrs.at[i], device_id=where, device_id_type=MESH)

    small[...] = jnp.zeros_like(small)
    for i in range(9):
        small[3 * i : 3 * i + 3, :chans] = dw[i // 3, i % 3]
    small[27:28, :chans] = bias[...]
    turned_small = small[...].T
    for i in range(28):
        taps[i] = jnp.broadcast_to(turned_small[:chans, i : i + 1], (chans, 128))
    small[...] = jnp.zeros_like(small)
    for x in range(rx):
        small[x * chans : (x + 1) * chans, x * chans : (x + 1) * chans] = pw[...]
    point[...] = left(small[...].T, 1)

    for i in range(len(tiles)):
        field_copy(i).wait()
    flat = raw.reshape(depth // 128, rx, chans * ry, 128)

    def forward(i, carry):
        data = []
        for yy in range(4):
            y = i * 4 + yy
            for x in range(rx):
                cell = jnp.concatenate(
                    [flat[h, x, pl.ds(y, chans, stride=ry), :] for h in range(depth // 128)], axis=1)
                pad[y + 1, x + 1] = cell
                data.append(cell)
        zspec = dot(zfwd[...], right(jnp.concatenate(data, axis=0), 1), ((1,), (1,)))
        for yy in range(4):
            for p in range(pieces):
                for g in range(gy):
                    at = (p * gy + g) * 2 * kc
                    row = pl.ds(pl.multiple_of((g * ry + i * 4 + yy) * 2 * kc, 8), 2 * kc)
                    zs[p, row, :] = zspec[at : at + 2 * kc, yy * lanes : (yy + 1) * lanes]
        return carry

    lax.fori_loop(0, ry // 4, forward, 0)

    pl.semaphore_wait(barrier, gx + gy - 2)
    for p in range(pieces):
        each(ycopy, gy, *zargs, p)

    def second(p, carry):
        keep_own(zs, zr, p, my, yblk)
        yall(*zargs, p).wait_recv()
        data = jnp.concatenate([
            jnp.concatenate([zr[p, pl.ds(r * kc + k, full_y, stride=2 * kc), :] for r in range(2)], axis=0)
            for k in range(kc)], axis=1)
        yspec = dot(yfwd[...], right(data, 0))
        for k in range(kc):
            ys[p, pl.ds(k, 2 * modes, stride=kc), :] = yspec[:, k * lanes : (k + 1) * lanes]
        each(xcopy, gx, *yargs, p)
        keep_own(ys, yr, p, mx, xblk)
        return carry

    lax.fori_loop(0, pieces, second, 0)

    def local_part(y, carry):
        here = pad[y + 1, pl.ds(1, rx)].reshape(lanes, depth)
        base = dot(point[...], right(here, 0))
        for cc in range(0, chans, 8):
            sums = [[None] * 3 for _ in range(rx)]
            for b in range(3):
                for xp in range(rx + 2):
                    value = pad[y + b, xp, cc : cc + 8, :]
                    for a in range(3):
                        x = xp - a
                        if 0 <= x < rx:
                            for e in range(3):
                                tap = taps[(a * 3 + b) * 3 + e, cc : cc + 8, :]
                                term = jnp.concatenate([tap] * (depth // 128), axis=1) * value
                                sums[x][e] = term if sums[x][e] is None else sums[x][e] + term
            shift = jnp.concatenate([taps[27, cc : cc + 8, :]] * (depth // 128), axis=1)
            for x in range(rx):
                total = sums[x][1] + pltpu.roll(sums[x][0], 1, 1) + pltpu.roll(sums[x][2], depth - 1, 1)
                acc[y, x, cc : cc + 8, :] = total + base[x * chans + cc : x * chans + cc + 8, :] + shift
        return carry

    def channels(p, before):
        xall(*yargs, p).wait_recv()

        @pl.when(p == 0)
        def _():
            halo(0).start()
            halo(1).start()

        gathered = []
        for g in range(groups):
            nl, q = g // quads, g % quads
            data = [
                jnp.concatenate(
                    [yr[p, pl.ds((nl * 2 + s) * kc + q * 4 + j, gx, stride=xblk), :] for s in range(2)], axis=0)
                for j in range(4)]
            gathered.append(jnp.concatenate([
                jnp.concatenate([part[:, x * chans : (x + 1) * chans] for part in data], axis=1)
                for x in range(rx)], axis=0))
        wide = dot(xfwd[...], right(jnp.concatenate(gathered, axis=1), 0))
        span = 4 * chans
        shape = (8 * modes, span)
        own = lax.rem(lax.broadcasted_iota(jnp.int32, shape, 0), 4) == lax.broadcasted_iota(jnp.int32, shape, 1) // chans
        for g in range(groups):
            for r in range(2):
                kept_part = jnp.where(own, wide[r * 8 * modes : (r + 1) * 8 * modes, g * span : (g + 1) * span], 0.0)
                high = kept_part.astype(jnp.bfloat16).astype(jnp.float32)
                both = jnp.concatenate(
                    [high.reshape(modes, 8, span), (kept_part - high).reshape(modes, 8, span)], axis=1)
                spec[g, :, r * span : (r + 1) * span] = both.reshape(16 * modes, span).astype(jnp.bfloat16)
        weight_copy(p).wait()

        def mix(g, carry):
            nl, q = g // quads, g % quads
            for m in range(modes):
                block_w = jnp.concatenate(
                    [weight[r, m, nl, p * kc + q * 4 + j] for r in range(2) for j in range(4)], axis=0)
                high, low = halves(block_w)
                rows = spec[g, m * 16 : (m + 1) * 16, :]
                total = dot(jnp.concatenate([rows, rows], axis=1), jnp.concatenate([high, low], axis=0))
                parts[g, m * 8 : (m + 1) * 8, :] = total[:8] + total[8:]
            return carry

        lax.fori_loop(0, groups, mix, 0)
        back = dot(xback[...], right(jnp.concatenate([parts[g] for g in range(groups)], axis=1), 0))
        for g in range(groups):
            nl, q = g // quads, g % quads
            for j in range(4):
                for s in range(2):
                    at = (j * rx * 2 + s) * gx
                    ms[p, pl.ds((nl * 2 + s) * kc + q * 4 + j, gx, stride=xblk), :] = jnp.concatenate(
                        [back[at + x * 2 * gx : at + (x * 2 + 1) * gx, g * chans : (g + 1) * chans]
                         for x in range(rx)], axis=1)
        each(xcopy, gx, *margs, p)
        keep_own(ms, mr, p, mx, xblk)

        @pl.when(p == 0)
        def _():
            halo(0).wait_recv()
            halo(1).wait_recv()
            halo(2).start()
            halo(3).start()

        return before

    lax.fori_loop(0, pieces, channels, 0)

    halo(2).wait_recv()
    halo(3).wait_recv()
    lax.fori_loop(0, ry, local_part, 0)

    def second_back(p, carry):
        xall(*margs, p).wait_recv()
        data = jnp.concatenate([mr[p, pl.ds(k, 2 * modes, stride=kc), :] for k in range(kc)], axis=1)
        tall = dot(yback[...], right(data, 0))
        for k in range(kc):
            ts[p, pl.ds(k, 2 * full_y, stride=kc), :] = tall[:, k * lanes : (k + 1) * lanes]
        each(ycopy, gy, *targs, p)
        keep_own(ts, tr, p, my, yblk)
        return carry

    lax.fori_loop(0, pieces, second_back, 0)
    for p in range(pieces):
        yall(*targs, p).wait_recv()

    def finish(i, carry):
        data = jnp.concatenate([
            jnp.concatenate([
                tr[p, pl.ds(pl.multiple_of((g * ry + i * 4 + yy) * 2 * kc, 8), 2 * kc), :]
                for p in range(pieces) for g in range(gy)], axis=0)
            for yy in range(4)], axis=1)
        spectral = dot(left(data, 0), zback[...], ((0,), (0,)))
        for yy in range(4):
            y = i * 4 + yy
            for x in range(rx):
                at = yy * lanes + x * chans
                total = spectral[at : at + chans] + acc[y, x]
                for h in range(depth // 128):
                    flat[h, x, pl.ds(y, chans, stride=ry), :] = total[:, h * 128 : (h + 1) * 128]
        return carry

    lax.fori_loop(0, ry // 4, finish, 0)

    def out_copy(i):
        h, x = tiles[i]
        return pltpu.make_async_copy(raw.at[h, x], out_hbm.at[:, x, :, pl.ds(h * 128, 128)], fsem.at[i])

    for i in range(len(tiles)):
        out_copy(i).start()
    for i in range(4):
        halo(i).wait_send()
    for p in range(pieces):
        yall(*zargs, p).wait_send()
        xall(*yargs, p).wait_send()
        xall(*margs, p).wait_send()
        yall(*targs, p).wait_send()
    for i in range(len(tiles)):
        out_copy(i).wait()


def on_device(field, spec_weight, dw_kernel, point_weight, bias):
    gx, gy = lax.axis_size("gx"), lax.axis_size("gy")
    chans, rx, ry, depth = field.shape
    modes, nlc, kl = spec_weight.shape[1:4]
    lanes = rx * chans
    f32 = jnp.float32
    pieces = 2 if kl % 8 == 0 else 1
    kc = kl // pieces
    cfg = (gx, gy, rx, ry, depth, modes, pieces)

    vmem = pl.BlockSpec(memory_space=pltpu.VMEM)
    hbm = pl.BlockSpec(memory_space=pl.ANY)
    ybuf = pltpu.VMEM((pieces, gy * ry * 2 * kc, lanes), f32)
    xbuf = pltpu.VMEM((pieces, gx * nlc * 2 * kc, lanes), f32)
    dma = pltpu.SemaphoreType.DMA
    out = pl.pallas_call(
        functools.partial(layer_kernel, cfg),
        in_specs=[vmem] * 9 + [hbm] * 2,
        out_specs=hbm,
        out_shape=jax.ShapeDtypeStruct(field.shape, f32),
        scratch_shapes=[
            pltpu.VMEM(spec_weight.shape, f32),
            pltpu.VMEM((ry + 2, rx + 2, chans, depth), f32),
            pltpu.VMEM((depth // 128, rx, chans, ry, 128), f32),
            pltpu.VMEM((ry, rx, chans, depth), f32),
            pltpu.VMEM((28, chans, 128), f32),
            pltpu.VMEM((lanes, lanes), f32),
            pltpu.VMEM((lanes, 3 * lanes), jnp.bfloat16),
            ybuf, ybuf, xbuf, xbuf, xbuf, xbuf, ybuf, ybuf,
            pltpu.VMEM((nlc * kc // 4, 16 * modes, 8 * chans), jnp.bfloat16),
            pltpu.VMEM((nlc * kc // 4, 8 * modes, chans), f32),
            dma((rx * depth // 128,)), dma((pieces,)),
            dma((pieces,)), dma((pieces,)), dma((pieces,)), dma((pieces,)),
            dma((pieces,)), dma((pieces,)), dma((pieces,)), dma((pieces,)),
            dma((4,)), dma((4,)),
        ],
        compiler_params=params(60, collective_id=0, has_side_effects=True),
        name="layer",
    )(*tables(cfg), jnp.transpose(dw_kernel, (1, 2, 3, 0)), point_weight, bias[None], field, spec_weight)
    return jax.nn.gelu(out)


def solution(mesh):
    placed = (P(None, "gx", "gy", None), P(None, None, "gx", "gy", None, None), P(), P(), P())
    return jax.shard_map(
        on_device, mesh=mesh, in_specs=placed, out_specs=P(None, "gx", "gy", None), check_vma=False
    )
```

```python
import functools

import jax
import jax.numpy as jnp
import ml_dtypes
import numpy as np
from jax import lax
from jax.experimental import pallas as pl
from jax.experimental.pallas import tpu as pltpu
from jax.sharding import PartitionSpec as P

MIB = 1 << 20


def params(mib, **more):
    return pltpu.CompilerParams(vmem_limit_bytes=mib * MIB, **more)


def halves(a):
    high = a.astype(jnp.bfloat16)
    return high, (a - high.astype(jnp.float32)).astype(jnp.bfloat16)


def left(a, axis):
    high, low = halves(a)
    return jnp.concatenate([high, low, high], axis=axis)


def right(a, axis):
    high, low = halves(a)
    return jnp.concatenate([high, high, low], axis=axis)


def table_halves(a):
    high = a.astype(ml_dtypes.bfloat16)
    return high, (a - high.astype(np.float32)).astype(ml_dtypes.bfloat16)


def table_left(a):
    high, low = table_halves(a)
    return np.concatenate([high, low, high], axis=1)


def table_right(a):
    high, low = table_halves(a)
    return np.concatenate([high, high, low], axis=0)


def dot(a, b, dims=((1,), (0,))):
    return lax.dot_general(a, b, (dims, ((), ())), preferred_element_type=jnp.float32)


def kept(modes, length):
    index = np.arange(modes)
    return np.where(index < modes // 2, index, index + length - modes)


def waves(freqs, length):
    angle = (freqs[:, None] * np.arange(length)[None, :] % length) * (2.0 * np.pi / length)
    return np.cos(angle), np.sin(angle)


def table_pair(modes, length, direction):
    cosine, sine = waves(kept(modes, length), length)
    upper = np.stack([cosine, direction * sine])
    lower = np.stack([-direction * sine, cosine])
    return np.stack([upper, lower])


def rows_z(modes, depth, groups, pieces, table):
    kc = modes // (groups * pieces)
    return table.reshape(2, groups, pieces, kc, depth).transpose(2, 1, 0, 3, 4).reshape(2 * modes, depth).astype(np.float32)


def tables(cfg):
    gx, gy, rx, ry, depth, modes, pieces = cfg
    full_x, full_y = rx * gx, ry * gy
    cosine, sine = waves(np.arange(modes), depth)
    zfwd = rows_z(modes, depth, gy, pieces, np.stack([cosine, -sine]))
    weight = (np.where(np.arange(modes) == 0, 1.0, 2.0) / depth)[:, None]
    zback = rows_z(modes, depth, gy, pieces, np.stack([weight * cosine, -weight * sine]))
    yfwd = table_pair(modes, full_y, 1.0).transpose(2, 0, 1, 3).reshape(2 * modes, 2 * full_y).astype(np.float32)
    yback = (table_pair(modes, full_y, -1.0) / full_y).transpose(3, 0, 2, 1)
    yback = yback.reshape(2 * full_y, 2 * modes).astype(np.float32)
    xtab = table_pair(modes, full_x, 1.0).reshape(2, 2, modes, gx, rx)
    factor = np.stack([np.stack([xtab[0], xtab[1]]), np.stack([-xtab[1], xtab[0]])])
    xfwd = factor.transpose(0, 3, 1, 5, 2, 4).reshape(4 * modes, rx * 2 * gx)
    xfwd = np.repeat(xfwd, 4, axis=0)
    xtab = (table_pair(modes, full_x, -1.0) / full_x).reshape(2, 2, modes, gx, rx).transpose(4, 0, 3, 2, 1)
    xback = np.zeros((4, rx, 2, gx, modes, 2, 4), np.float32)
    for j in range(4):
        xback[j, ..., j] = xtab
    xback = xback.reshape(4 * rx * 2 * gx, 8 * modes)
    return (table_left(zfwd), table_left(yfwd), table_left(xfwd), table_left(xback), table_left(yback),
            table_right(zback))


def layer_kernel(cfg, zfwd, yfwd, xfwd, xback, yback, zback, dw, pw, bias, field_hbm, weight_hbm, out_hbm,
                 weight, pad, raw, edges, acc, taps, small, point, zs, zr, ys, yr, ms, mr, ts, tr, spec, parts,
                 fsem, wsem, zss, zrs, yss, yrs, mss, mrs, tss, trs, hss, hrs):
    gx, gy, rx, ry, depth, modes, pieces = cfg
    chans = pad.shape[2]
    lanes = rx * chans
    full_y = ry * gy
    nlc, kl = weight.shape[2:4]
    kc = kl // pieces
    quads = kc // 4
    groups = nlc * quads
    xblk = nlc * 2 * kc
    yblk = ry * 2 * kc
    mx, my = lax.axis_index("gx"), lax.axis_index("gy")
    MESH = pl.DeviceIdType.MESH

    def weight_copy(p):
        at = pl.ds(p * kc, kc)
        return pltpu.make_async_copy(weight_hbm.at[:, :, :, at], weight.at[:, :, :, at], wsem.at[p])

    tiles = [(h, x) for x in range(rx) for h in range(depth // 128)]

    def field_copy(i):
        h, x = tiles[i]
        return pltpu.make_async_copy(field_hbm.at[:, x, :, pl.ds(h * 128, 128)], raw.at[h, x], fsem.at[i])

    for i in range(len(tiles)):
        field_copy(i).start()
    for p in range(pieces):
        weight_copy(p).start()

    barrier = pltpu.get_barrier_semaphore()
    for d in range(1, gx):
        pl.semaphore_signal(barrier, inc=1, device_id=(lax.rem(mx + d, gx), my), device_id_type=MESH)
    for d in range(1, gy):
        pl.semaphore_signal(barrier, inc=1, device_id=(mx, lax.rem(my + d, gy)), device_id_type=MESH)

    def block(ref, p, at, rows):
        return ref.at[p, pl.ds(pl.multiple_of(at * rows, 8), rows)]

    def xcopy(src, dst, ssem, rsem, p, i):
        half = (i + 1) // 2
        to = lax.rem(mx + gx // 2 + half * (1 - 2 * lax.rem(i, 2)) + gx, gx)
        return pltpu.make_async_remote_copy(
            src_ref=block(src, p, to, xblk), dst_ref=block(dst, p, mx, xblk), send_sem=ssem.at[p],
            recv_sem=rsem.at[p], device_id=(to, my), device_id_type=MESH)

    def ycopy(src, dst, ssem, rsem, p, d):
        to = lax.rem(my + d + 1, gy)
        return pltpu.make_async_remote_copy(
            src_ref=block(src, p, to, yblk), dst_ref=block(dst, p, my, yblk), send_sem=ssem.at[p],
            recv_sem=rsem.at[p], device_id=(mx, to), device_id_type=MESH)

    def xall(src, dst, ssem, rsem, p):
        rows = pl.ds(0, (gx - 1) * xblk)
        return pltpu.make_async_remote_copy(
            src_ref=src.at[p, rows], dst_ref=dst.at[p, rows], send_sem=ssem.at[p], recv_sem=rsem.at[p],
            device_id=(lax.rem(mx + 1, gx), my), device_id_type=MESH)

    def yall(src, dst, ssem, rsem, p):
        rows = pl.ds(0, (gy - 1) * yblk)
        return pltpu.make_async_remote_copy(
            src_ref=src.at[p, rows], dst_ref=dst.at[p, rows], send_sem=ssem.at[p], recv_sem=rsem.at[p],
            device_id=(mx, lax.rem(my + 1, gy)), device_id_type=MESH)

    def each(make, count, *args):
        def step(i, carry):
            make(*args, i).start()
            return carry
        lax.fori_loop(0, count - 1, step, 0)

    zargs, yargs = (zs, zr, zss, zrs), (ys, yr, yss, yrs)
    margs, targs = (ms, mr, mss, mrs), (ts, tr, tss, trs)

    def keep_own(src, dst, p, at, rows):
        own = pl.ds(pl.multiple_of(at * rows, 8), rows)
        dst[p, own, :] = src[p, own, :]

    def halo(i):
        if i < 2:
            to = lax.rem(mx + (1 if i == 0 else gx - 1), gx)
            src = raw.at[:, rx - 1 if i == 0 else 0]
            dst = edges.at[i]
            where = (to, my)
        else:
            to = lax.rem(my + (1 if i == 2 else gy - 1), gy)
            src = pad.at[pl.ds(ry if i == 2 else 1, 1)]
            dst = pad.at[pl.ds(0 if i == 2 else ry + 1, 1)]
            where = (mx, to)
        return pltpu.make_async_remote_copy(
            src_ref=src, dst_ref=dst, send_sem=hss.at[i], recv_sem=hrs.at[i], device_id=where, device_id_type=MESH)

    small[...] = jnp.zeros_like(small)
    for i in range(9):
        small[3 * i : 3 * i + 3, :chans] = dw[i // 3, i % 3]
    small[27:28, :chans] = bias[...]
    turned_small = small[...].T
    for i in range(28):
        taps[i] = jnp.broadcast_to(turned_small[:chans, i : i + 1], (chans, 128))
    small[...] = jnp.zeros_like(small)
    for x in range(rx):
        small[x * chans : (x + 1) * chans, x * chans : (x + 1) * chans] = pw[...]
    point[...] = left(small[...].T, 1)

    for i in range(len(tiles)):
        field_copy(i).wait()
    pl.semaphore_wait(barrier, gx + gy - 2)
    halo(0).start()
    halo(1).start()
    flat = raw.reshape(depth // 128, rx, chans * ry, 128)

    def forward(i, carry):
        data = []
        for yy in range(4):
            y = i * 4 + yy
            for x in range(rx):
                cell = jnp.concatenate(
                    [flat[h, x, pl.ds(y, chans, stride=ry), :] for h in range(depth // 128)], axis=1)
                pad[y + 1, x + 1] = cell
                data.append(cell)
        zspec = dot(zfwd[...], right(jnp.concatenate(data, axis=0), 1), ((1,), (1,)))
        for yy in range(4):
            for p in range(pieces):
                for g in range(gy):
                    at = (p * gy + g) * 2 * kc
                    row = pl.ds(pl.multiple_of((g * ry + i * 4 + yy) * 2 * kc, 8), 2 * kc)
                    zs[p, row, :] = zspec[at : at + 2 * kc, yy * lanes : (yy + 1) * lanes]
        return carry

    lax.fori_loop(0, ry // 4, forward, 0)

    for p in range(pieces):
        each(ycopy, gy, *zargs, p)

    def second(p, carry):
        keep_own(zs, zr, p, my, yblk)
        yall(*zargs, p).wait_recv()
        data = jnp.concatenate([
            jnp.concatenate([zr[p, pl.ds(r * kc + k, full_y, stride=2 * kc), :] for r in range(2)], axis=0)
            for k in range(kc)], axis=1)
        yspec = dot(yfwd[...], right(data, 0))
        for k in range(kc):
            ys[p, pl.ds(k, 2 * modes, stride=kc), :] = yspec[:, k * lanes : (k + 1) * lanes]
        each(xcopy, gx, *yargs, p)
        keep_own(ys, yr, p, mx, xblk)
        return carry

    lax.fori_loop(0, pieces, second, 0)

    for i in range(2):
        halo(i).wait_recv()
    flat_edges = edges.reshape(2, depth // 128, chans * ry, 128)

    def sides(y, carry):
        for i in range(2):
            pad[y + 1, 0 if i == 0 else rx + 1] = jnp.concatenate(
                [flat_edges[i, h, pl.ds(y, chans, stride=ry), :] for h in range(depth // 128)], axis=1)
        return carry

    lax.fori_loop(0, ry, sides, 0)
    halo(2).start()
    halo(3).start()

    def local_part(y, carry):
        here = pad[y + 1, pl.ds(1, rx)].reshape(lanes, depth)
        base = dot(point[...], right(here, 0))
        for cc in range(0, chans, 8):
            sums = [[None] * 3 for _ in range(rx)]
            for b in range(3):
                for xp in range(rx + 2):
                    value = pad[y + b, xp, cc : cc + 8, :]
                    for a in range(3):
                        x = xp - a
                        if 0 <= x < rx:
                            for e in range(3):
                                tap = taps[(a * 3 + b) * 3 + e, cc : cc + 8, :]
                                term = jnp.concatenate([tap] * (depth // 128), axis=1) * value
                                sums[x][e] = term if sums[x][e] is None else sums[x][e] + term
            shift = jnp.concatenate([taps[27, cc : cc + 8, :]] * (depth // 128), axis=1)
            for x in range(rx):
                total = sums[x][1] + pltpu.roll(sums[x][0], 1, 1) + pltpu.roll(sums[x][2], depth - 1, 1)
                acc[y, x, cc : cc + 8, :] = total + base[x * chans + cc : x * chans + cc + 8, :] + shift
        return carry

    lax.fori_loop(1, ry // 2, local_part, 0)

    def channels(p, before):
        xall(*yargs, p).wait_recv()
        gathered = []
        for g in range(groups):
            nl, q = g // quads, g % quads
            data = [
                jnp.concatenate(
                    [yr[p, pl.ds((nl * 2 + s) * kc + q * 4 + j, gx, stride=xblk), :] for s in range(2)], axis=0)
                for j in range(4)]
            gathered.append(jnp.concatenate([
                jnp.concatenate([part[:, x * chans : (x + 1) * chans] for part in data], axis=1)
                for x in range(rx)], axis=0))
        wide = dot(xfwd[...], right(jnp.concatenate(gathered, axis=1), 0))
        span = 4 * chans
        shape = (8 * modes, span)
        own = lax.rem(lax.broadcasted_iota(jnp.int32, shape, 0), 4) == lax.broadcasted_iota(jnp.int32, shape, 1) // chans
        for g in range(groups):
            for r in range(2):
                kept_part = jnp.where(own, wide[r * 8 * modes : (r + 1) * 8 * modes, g * span : (g + 1) * span], 0.0)
                high = kept_part.astype(jnp.bfloat16).astype(jnp.float32)
                both = jnp.concatenate(
                    [high.reshape(modes, 8, span), (kept_part - high).reshape(modes, 8, span)], axis=1)
                spec[g, :, r * span : (r + 1) * span] = both.reshape(16 * modes, span).astype(jnp.bfloat16)
        weight_copy(p).wait()

        def mix(g, carry):
            nl, q = g // quads, g % quads
            for m in range(modes):
                block_w = jnp.concatenate(
                    [weight[r, m, nl, p * kc + q * 4 + j] for r in range(2) for j in range(4)], axis=0)
                high, low = halves(block_w)
                rows = spec[g, m * 16 : (m + 1) * 16, :]
                total = dot(jnp.concatenate([rows, rows], axis=1), jnp.concatenate([high, low], axis=0))
                parts[g, m * 8 : (m + 1) * 8, :] = total[:8] + total[8:]
            return carry

        lax.fori_loop(0, groups, mix, 0)
        back = dot(xback[...], right(jnp.concatenate([parts[g] for g in range(groups)], axis=1), 0))
        for g in range(groups):
            nl, q = g // quads, g % quads
            for j in range(4):
                for s in range(2):
                    at = (j * rx * 2 + s) * gx
                    ms[p, pl.ds((nl * 2 + s) * kc + q * 4 + j, gx, stride=xblk), :] = jnp.concatenate(
                        [back[at + x * 2 * gx : at + (x * 2 + 1) * gx, g * chans : (g + 1) * chans]
                         for x in range(rx)], axis=1)
        each(xcopy, gx, *margs, p)
        keep_own(ms, mr, p, mx, xblk)
        return before

    lax.fori_loop(0, pieces, channels, 0)

    halo(2).wait_recv()
    halo(3).wait_recv()
    lax.fori_loop(ry // 2, ry + 1, lambda y, carry: local_part(lax.rem(y, ry), carry), 0)
    for i in range(2):
        halo(i).wait_send()

    def second_back(p, carry):
        xall(*margs, p).wait_recv()
        data = jnp.concatenate([mr[p, pl.ds(k, 2 * modes, stride=kc), :] for k in range(kc)], axis=1)
        tall = dot(yback[...], right(data, 0))
        for k in range(kc):
            ts[p, pl.ds(k, 2 * full_y, stride=kc), :] = tall[:, k * lanes : (k + 1) * lanes]
        each(ycopy, gy, *targs, p)
        keep_own(ts, tr, p, my, yblk)
        return carry

    lax.fori_loop(0, pieces, second_back, 0)
    for p in range(pieces):
        yall(*targs, p).wait_recv()

    def finish(i, carry):
        data = jnp.concatenate([
            jnp.concatenate([
                tr[p, pl.ds(pl.multiple_of((g * ry + i * 4 + yy) * 2 * kc, 8), 2 * kc), :]
                for p in range(pieces) for g in range(gy)], axis=0)
            for yy in range(4)], axis=1)
        spectral = dot(left(data, 0), zback[...], ((0,), (0,)))
        for yy in range(4):
            y = i * 4 + yy
            for x in range(rx):
                at = yy * lanes + x * chans
                total = spectral[at : at + chans] + acc[y, x]
                for h in range(depth // 128):
                    flat[h, x, pl.ds(y, chans, stride=ry), :] = total[:, h * 128 : (h + 1) * 128]
        return carry

    lax.fori_loop(0, ry // 4, finish, 0)

    def out_copy(i):
        h, x = tiles[i]
        return pltpu.make_async_copy(raw.at[h, x], out_hbm.at[:, x, :, pl.ds(h * 128, 128)], fsem.at[i])

    for i in range(len(tiles)):
        out_copy(i).start()
    for i in range(2, 4):
        halo(i).wait_send()
    for p in range(pieces):
        yall(*zargs, p).wait_send()
        xall(*yargs, p).wait_send()
        xall(*margs, p).wait_send()
        yall(*targs, p).wait_send()
    for i in range(len(tiles)):
        out_copy(i).wait()


def on_device(field, spec_weight, dw_kernel, point_weight, bias):
    gx, gy = lax.axis_size("gx"), lax.axis_size("gy")
    chans, rx, ry, depth = field.shape
    modes, nlc, kl = spec_weight.shape[1:4]
    lanes = rx * chans
    f32 = jnp.float32
    pieces = 2 if kl % 8 == 0 else 1
    kc = kl // pieces
    cfg = (gx, gy, rx, ry, depth, modes, pieces)

    vmem = pl.BlockSpec(memory_space=pltpu.VMEM)
    hbm = pl.BlockSpec(memory_space=pl.ANY)
    ybuf = pltpu.VMEM((pieces, gy * ry * 2 * kc, lanes), f32)
    xbuf = pltpu.VMEM((pieces, gx * nlc * 2 * kc, lanes), f32)
    dma = pltpu.SemaphoreType.DMA
    out = pl.pallas_call(
        functools.partial(layer_kernel, cfg),
        in_specs=[vmem] * 9 + [hbm] * 2,
        out_specs=hbm,
        out_shape=jax.ShapeDtypeStruct(field.shape, f32),
        scratch_shapes=[
            pltpu.VMEM(spec_weight.shape, f32),
            pltpu.VMEM((ry + 2, rx + 2, chans, depth), f32),
            pltpu.VMEM((depth // 128, rx, chans, ry, 128), f32),
            pltpu.VMEM((2, depth // 128, chans, ry, 128), f32),
            pltpu.VMEM((ry, rx, chans, depth), f32),
            pltpu.VMEM((28, chans, 128), f32),
            pltpu.VMEM((lanes, lanes), f32),
            pltpu.VMEM((lanes, 3 * lanes), jnp.bfloat16),
            ybuf, ybuf, xbuf, xbuf, xbuf, xbuf, ybuf, ybuf,
            pltpu.VMEM((nlc * kc // 4, 16 * modes, 8 * chans), jnp.bfloat16),
            pltpu.VMEM((nlc * kc // 4, 8 * modes, chans), f32),
            dma((rx * depth // 128,)), dma((pieces,)),
            dma((pieces,)), dma((pieces,)), dma((pieces,)), dma((pieces,)),
            dma((pieces,)), dma((pieces,)), dma((pieces,)), dma((pieces,)),
            dma((4,)), dma((4,)),
        ],
        compiler_params=params(60, collective_id=0, has_side_effects=True),
        name="layer",
    )(*tables(cfg), jnp.transpose(dw_kernel, (1, 2, 3, 0)), point_weight, bias[None], field, spec_weight)
    return jax.nn.gelu(out)


def solution(mesh):
    placed = (P(None, "gx", "gy", None), P(None, None, "gx", "gy", None, None), P(), P(), P())
    return jax.shard_map(
        on_device, mesh=mesh, in_specs=placed, out_specs=P(None, "gx", "gy", None), check_vma=False
    )
```

```python
import functools

import jax
import jax.numpy as jnp
import ml_dtypes
import numpy as np
from jax import lax
from jax.experimental import pallas as pl
from jax.experimental.pallas import tpu as pltpu
from jax.sharding import PartitionSpec as P

MIB = 1 << 20


def params(mib, **more):
    return pltpu.CompilerParams(vmem_limit_bytes=mib * MIB, **more)


def halves(a):
    high = a.astype(jnp.bfloat16)
    return high, (a - high.astype(jnp.float32)).astype(jnp.bfloat16)


def left(a, axis):
    high, low = halves(a)
    return jnp.concatenate([high, low, high], axis=axis)


def right(a, axis):
    high, low = halves(a)
    return jnp.concatenate([high, high, low], axis=axis)


def table_halves(a):
    high = a.astype(ml_dtypes.bfloat16)
    return high, (a - high.astype(np.float32)).astype(ml_dtypes.bfloat16)


def table_left(a):
    high, low = table_halves(a)
    return np.concatenate([high, low, high], axis=1)


def table_right(a):
    high, low = table_halves(a)
    return np.concatenate([high, high, low], axis=0)


def dot(a, b, dims=((1,), (0,))):
    return lax.dot_general(a, b, (dims, ((), ())), preferred_element_type=jnp.float32)


def kept(modes, length):
    index = np.arange(modes)
    return np.where(index < modes // 2, index, index + length - modes)


def waves(freqs, length):
    angle = (freqs[:, None] * np.arange(length)[None, :] % length) * (2.0 * np.pi / length)
    return np.cos(angle), np.sin(angle)


def table_pair(modes, length, direction):
    cosine, sine = waves(kept(modes, length), length)
    upper = np.stack([cosine, direction * sine])
    lower = np.stack([-direction * sine, cosine])
    return np.stack([upper, lower])


def rows_z(modes, depth, groups, pieces, table):
    kc = modes // (groups * pieces)
    return table.reshape(2, groups, pieces, kc, depth).transpose(2, 1, 0, 3, 4).reshape(2 * modes, depth).astype(np.float32)


def tables(cfg):
    gx, gy, rx, ry, depth, modes, pieces = cfg
    full_x, full_y = rx * gx, ry * gy
    cosine, sine = waves(np.arange(modes), depth)
    zfwd = rows_z(modes, depth, gy, pieces, np.stack([cosine, -sine]))
    weight = (np.where(np.arange(modes) == 0, 1.0, 2.0) / depth)[:, None]
    zback = rows_z(modes, depth, gy, pieces, np.stack([weight * cosine, -weight * sine]))
    yfwd = table_pair(modes, full_y, 1.0).transpose(2, 0, 1, 3).reshape(2 * modes, 2 * full_y).astype(np.float32)
    yback = (table_pair(modes, full_y, -1.0) / full_y).transpose(3, 0, 2, 1)
    yback = yback.reshape(2 * full_y, 2 * modes).astype(np.float32)
    xtab = table_pair(modes, full_x, 1.0).reshape(2, 2, modes, gx, rx)
    factor = np.stack([np.stack([xtab[0], xtab[1]]), np.stack([-xtab[1], xtab[0]])])
    xfwd = factor.transpose(0, 3, 1, 5, 2, 4).reshape(4 * modes, rx * 2 * gx)
    xfwd = np.repeat(xfwd, 4, axis=0)
    xtab = (table_pair(modes, full_x, -1.0) / full_x).reshape(2, 2, modes, gx, rx).transpose(4, 0, 3, 2, 1)
    xback = np.zeros((4, rx, 2, gx, modes, 2, 4), np.float32)
    for j in range(4):
        xback[j, ..., j] = xtab
    xback = xback.reshape(4 * rx * 2 * gx, 8 * modes)
    return (table_left(zfwd), table_left(yfwd), table_left(xfwd), table_left(xback), table_left(yback),
            table_right(zback))


def layer_kernel(cfg, zfwd, yfwd, xfwd, xback, yback, zback, dw, pw, bias, field_hbm, weight_hbm, out_hbm,
                 weight, pad, raw, edges, acc, taps, small, point, zs, zr, ys, yr, ms, mr, ts, tr, spec, parts,
                 fsem, wsem, zss, zrs, yss, yrs, mss, mrs, tss, trs, hss, hrs):
    gx, gy, rx, ry, depth, modes, pieces = cfg
    chans = pad.shape[2]
    lanes = rx * chans
    full_y = ry * gy
    nlc, kl = weight.shape[2:4]
    kc = kl // pieces
    quads = kc // 4
    groups = nlc * quads
    xblk = nlc * 2 * kc
    yblk = ry * 2 * kc
    mx, my = lax.axis_index("gx"), lax.axis_index("gy")
    MESH = pl.DeviceIdType.MESH

    def weight_copy(p):
        at = pl.ds(p * kc, kc)
        return pltpu.make_async_copy(weight_hbm.at[:, :, :, at], weight.at[:, :, :, at], wsem.at[p])

    tiles = [(h, x) for x in range(rx) for h in range(depth // 128)]

    def field_copy(i):
        h, x = tiles[i]
        return pltpu.make_async_copy(field_hbm.at[:, x, :, pl.ds(h * 128, 128)], raw.at[h, x], fsem.at[i])

    for i in range(len(tiles)):
        field_copy(i).start()
    for p in range(pieces):
        weight_copy(p).start()

    barrier = pltpu.get_barrier_semaphore()
    for d in range(1, gx):
        pl.semaphore_signal(barrier, inc=1, device_id=(lax.rem(mx + d, gx), my), device_id_type=MESH)
    for d in range(1, gy):
        pl.semaphore_signal(barrier, inc=1, device_id=(mx, lax.rem(my + d, gy)), device_id_type=MESH)

    def block(ref, p, at, rows):
        return ref.at[p, pl.ds(pl.multiple_of(at * rows, 8), rows)]

    def xcopy(src, dst, ssem, rsem, p, i):
        half = (i + 1) // 2
        to = lax.rem(mx + gx // 2 + half * (1 - 2 * lax.rem(i, 2)) + gx, gx)
        return pltpu.make_async_remote_copy(
            src_ref=block(src, p, to, xblk), dst_ref=block(dst, p, mx, xblk), send_sem=ssem.at[p],
            recv_sem=rsem.at[p], device_id=(to, my), device_id_type=MESH)

    def ycopy(src, dst, ssem, rsem, p, d):
        to = lax.rem(my + d + 1, gy)
        return pltpu.make_async_remote_copy(
            src_ref=block(src, p, to, yblk), dst_ref=block(dst, p, my, yblk), send_sem=ssem.at[p],
            recv_sem=rsem.at[p], device_id=(mx, to), device_id_type=MESH)

    def xall(src, dst, ssem, rsem, p):
        rows = pl.ds(0, (gx - 1) * xblk)
        return pltpu.make_async_remote_copy(
            src_ref=src.at[p, rows], dst_ref=dst.at[p, rows], send_sem=ssem.at[p], recv_sem=rsem.at[p],
            device_id=(lax.rem(mx + 1, gx), my), device_id_type=MESH)

    def yall(src, dst, ssem, rsem, p):
        rows = pl.ds(0, (gy - 1) * yblk)
        return pltpu.make_async_remote_copy(
            src_ref=src.at[p, rows], dst_ref=dst.at[p, rows], send_sem=ssem.at[p], recv_sem=rsem.at[p],
            device_id=(mx, lax.rem(my + 1, gy)), device_id_type=MESH)

    def each(make, count, *args):
        def step(i, carry):
            make(*args, i).start()
            return carry
        lax.fori_loop(0, count - 1, step, 0)

    zargs, yargs = (zs, zr, zss, zrs), (ys, yr, yss, yrs)
    margs, targs = (ms, mr, mss, mrs), (ts, tr, tss, trs)

    def keep_own(src, dst, p, at, rows):
        own = pl.ds(pl.multiple_of(at * rows, 8), rows)
        dst[p, own, :] = src[p, own, :]

    def halo(i):
        if i < 2:
            to = lax.rem(mx + (1 if i == 0 else gx - 1), gx)
            src = raw.at[:, rx - 1 if i == 0 else 0]
            dst = edges.at[i]
            where = (to, my)
        else:
            to = lax.rem(my + (1 if i == 2 else gy - 1), gy)
            src = pad.at[pl.ds(ry if i == 2 else 1, 1)]
            dst = pad.at[pl.ds(0 if i == 2 else ry + 1, 1)]
            where = (mx, to)
        return pltpu.make_async_remote_copy(
            src_ref=src, dst_ref=dst, send_sem=hss.at[i], recv_sem=hrs.at[i], device_id=where, device_id_type=MESH)

    small[...] = jnp.zeros_like(small)
    for i in range(9):
        small[3 * i : 3 * i + 3, :chans] = dw[i // 3, i % 3]
    small[27:28, :chans] = bias[...]
    turned_small = small[...].T
    for i in range(28):
        taps[i] = jnp.broadcast_to(turned_small[:chans, i : i + 1], (chans, 128))
    small[...] = jnp.zeros_like(small)
    for x in range(rx):
        small[x * chans : (x + 1) * chans, x * chans : (x + 1) * chans] = pw[...]
    point[...] = left(small[...].T, 1)

    for i in range(len(tiles)):
        field_copy(i).wait()
    pl.semaphore_wait(barrier, gx + gy - 2)
    halo(0).start()
    halo(1).start()
    flat = raw.reshape(depth // 128, rx, chans * ry, 128)

    def forward(i, carry):
        data = []
        for yy in range(4):
            y = i * 4 + yy
            for x in range(rx):
                cell = jnp.concatenate(
                    [flat[h, x, pl.ds(y, chans, stride=ry), :] for h in range(depth // 128)], axis=1)
                pad[y + 1, x + 1] = cell
                data.append(cell)
        zspec = dot(zfwd[...], right(jnp.concatenate(data, axis=0), 1), ((1,), (1,)))
        for yy in range(4):
            for p in range(pieces):
                for g in range(gy):
                    at = (p * gy + g) * 2 * kc
                    row = pl.ds(pl.multiple_of((g * ry + i * 4 + yy) * 2 * kc, 8), 2 * kc)
                    zs[p, row, :] = zspec[at : at + 2 * kc, yy * lanes : (yy + 1) * lanes]
        return carry

    lax.fori_loop(0, ry // 4, forward, 0)

    for p in range(pieces):
        each(ycopy, gy, *zargs, p)

    def second(p, carry):
        keep_own(zs, zr, p, my, yblk)
        yall(*zargs, p).wait_recv()
        data = jnp.concatenate([
            jnp.concatenate([zr[p, pl.ds(r * kc + k, full_y, stride=2 * kc), :] for r in range(2)], axis=0)
            for k in range(kc)], axis=1)
        yspec = dot(yfwd[...], right(data, 0))
        for k in range(kc):
            ys[p, pl.ds(k, 2 * modes, stride=kc), :] = yspec[:, k * lanes : (k + 1) * lanes]
        each(xcopy, gx, *yargs, p)
        keep_own(ys, yr, p, mx, xblk)
        return carry

    lax.fori_loop(0, pieces, second, 0)

    for i in range(2):
        halo(i).wait_recv()
    flat_edges = edges.reshape(2, depth // 128, chans * ry, 128)

    def sides(y, carry):
        for i in range(2):
            pad[y + 1, 0 if i == 0 else rx + 1] = jnp.concatenate(
                [flat_edges[i, h, pl.ds(y, chans, stride=ry), :] for h in range(depth // 128)], axis=1)
        return carry

    lax.fori_loop(0, ry, sides, 0)
    halo(2).start()
    halo(3).start()

    def local_part(y, carry):
        here = pad[y + 1, pl.ds(1, rx)].reshape(lanes, depth)
        base = dot(point[...], right(here, 0))
        for cc in range(0, chans, 8):
            sums = [[None] * 3 for _ in range(rx)]
            for b in range(3):
                for xp in range(rx + 2):
                    value = pad[y + b, xp, cc : cc + 8, :]
                    for a in range(3):
                        x = xp - a
                        if 0 <= x < rx:
                            for e in range(3):
                                tap = taps[(a * 3 + b) * 3 + e, cc : cc + 8, :]
                                term = jnp.concatenate([tap] * (depth // 128), axis=1) * value
                                sums[x][e] = term if sums[x][e] is None else sums[x][e] + term
            shift = jnp.concatenate([taps[27, cc : cc + 8, :]] * (depth // 128), axis=1)
            for x in range(rx):
                total = sums[x][1] + pltpu.roll(sums[x][0], 1, 1) + pltpu.roll(sums[x][2], depth - 1, 1)
                acc[y, x, cc : cc + 8, :] = total + base[x * chans + cc : x * chans + cc + 8, :] + shift
        return carry

    lax.fori_loop(1, ry // 2, local_part, 0)

    def channels(p, before):
        xall(*yargs, p).wait_recv()
        gathered = []
        for g in range(groups):
            nl, q = g // quads, g % quads
            data = [
                jnp.concatenate(
                    [yr[p, pl.ds((nl * 2 + s) * kc + q * 4 + j, gx, stride=xblk), :] for s in range(2)], axis=0)
                for j in range(4)]
            gathered.append(jnp.concatenate([
                jnp.concatenate([part[:, x * chans : (x + 1) * chans] for part in data], axis=1)
                for x in range(rx)], axis=0))
        wide = dot(xfwd[...], right(jnp.concatenate(gathered, axis=1), 0))
        span = 4 * chans
        shape = (8 * modes, span)
        own = lax.rem(lax.broadcasted_iota(jnp.int32, shape, 0), 4) == lax.broadcasted_iota(jnp.int32, shape, 1) // chans
        for g in range(groups):
            for r in range(2):
                kept_part = jnp.where(own, wide[r * 8 * modes : (r + 1) * 8 * modes, g * span : (g + 1) * span], 0.0)
                high = kept_part.astype(jnp.bfloat16).astype(jnp.float32)
                both = jnp.concatenate(
                    [high.reshape(modes, 8, span), (kept_part - high).reshape(modes, 8, span)], axis=1)
                spec[g, :, r * span : (r + 1) * span] = both.reshape(16 * modes, span).astype(jnp.bfloat16)
        weight_copy(p).wait()

        def mix(g, carry):
            nl, q = g // quads, g % quads
            for m in range(modes):
                block_w = jnp.concatenate(
                    [weight[r, m, nl, p * kc + q * 4 + j] for r in range(2) for j in range(4)], axis=0)
                high, low = halves(block_w)
                rows = spec[g, m * 16 : (m + 1) * 16, :]
                total = dot(jnp.concatenate([rows, rows], axis=1), jnp.concatenate([high, low], axis=0))
                parts[g, m * 8 : (m + 1) * 8, :] = total[:8] + total[8:]
            return carry

        lax.fori_loop(0, groups, mix, 0)
        back = dot(xback[...], right(jnp.concatenate([parts[g] for g in range(groups)], axis=1), 0))
        for g in range(groups):
            nl, q = g // quads, g % quads
            for j in range(4):
                for s in range(2):
                    at = (j * rx * 2 + s) * gx
                    ms[p, pl.ds((nl * 2 + s) * kc + q * 4 + j, gx, stride=xblk), :] = jnp.concatenate(
                        [back[at + x * 2 * gx : at + (x * 2 + 1) * gx, g * chans : (g + 1) * chans]
                         for x in range(rx)], axis=1)
        each(xcopy, gx, *margs, p)
        keep_own(ms, mr, p, mx, xblk)
        return before

    lax.fori_loop(0, pieces, channels, 0)

    halo(2).wait_recv()
    halo(3).wait_recv()
    lax.fori_loop(ry // 2, ry + 1, lambda y, carry: local_part(lax.rem(y, ry), carry), 0)
    for i in range(2):
        halo(i).wait_send()

    def second_back(p, carry):
        xall(*margs, p).wait_recv()
        data = jnp.concatenate([mr[p, pl.ds(k, 2 * modes, stride=kc), :] for k in range(kc)], axis=1)
        tall = dot(yback[...], right(data, 0))
        for k in range(kc):
            ts[p, pl.ds(k, 2 * full_y, stride=kc), :] = tall[:, k * lanes : (k + 1) * lanes]
        each(ycopy, gy, *targs, p)
        keep_own(ts, tr, p, my, yblk)
        return carry

    lax.fori_loop(0, pieces, second_back, 0)
    for p in range(pieces):
        yall(*targs, p).wait_recv()

    def finish(i, carry):
        data = jnp.concatenate([
            jnp.concatenate([
                tr[p, pl.ds(pl.multiple_of((g * ry + i * 4 + yy) * 2 * kc, 8), 2 * kc), :]
                for p in range(pieces) for g in range(gy)], axis=0)
            for yy in range(4)], axis=1)
        spectral = dot(left(data, 0), zback[...], ((0,), (0,)))
        for yy in range(4):
            y = i * 4 + yy
            for x in range(rx):
                at = yy * lanes + x * chans
                total = spectral[at : at + chans] + acc[y, x]
                for h in range(depth // 128):
                    flat[h, x, pl.ds(y, chans, stride=ry), :] = total[:, h * 128 : (h + 1) * 128]
        return carry

    lax.fori_loop(0, ry // 4, finish, 0)

    def out_copy(i):
        h, x = tiles[i]
        return pltpu.make_async_copy(raw.at[h, x], out_hbm.at[:, x, :, pl.ds(h * 128, 128)], fsem.at[i])

    for i in range(len(tiles)):
        out_copy(i).start()
    for i in range(2, 4):
        halo(i).wait_send()
    for p in range(pieces):
        yall(*zargs, p).wait_send()
        xall(*yargs, p).wait_send()
        xall(*margs, p).wait_send()
        yall(*targs, p).wait_send()
    for i in range(len(tiles)):
        out_copy(i).wait()


def on_device(field, spec_weight, dw_kernel, point_weight, bias):
    gx, gy = lax.axis_size("gx"), lax.axis_size("gy")
    chans, rx, ry, depth = field.shape
    modes, nlc, kl = spec_weight.shape[1:4]
    lanes = rx * chans
    f32 = jnp.float32
    pieces = 4 if kl % 16 == 0 else 2 if kl % 8 == 0 else 1
    kc = kl // pieces
    cfg = (gx, gy, rx, ry, depth, modes, pieces)

    vmem = pl.BlockSpec(memory_space=pltpu.VMEM)
    hbm = pl.BlockSpec(memory_space=pl.ANY)
    ybuf = pltpu.VMEM((pieces, gy * ry * 2 * kc, lanes), f32)
    xbuf = pltpu.VMEM((pieces, gx * nlc * 2 * kc, lanes), f32)
    dma = pltpu.SemaphoreType.DMA
    out = pl.pallas_call(
        functools.partial(layer_kernel, cfg),
        in_specs=[vmem] * 9 + [hbm] * 2,
        out_specs=hbm,
        out_shape=jax.ShapeDtypeStruct(field.shape, f32),
        scratch_shapes=[
            pltpu.VMEM(spec_weight.shape, f32),
            pltpu.VMEM((ry + 2, rx + 2, chans, depth), f32),
            pltpu.VMEM((depth // 128, rx, chans, ry, 128), f32),
            pltpu.VMEM((2, depth // 128, chans, ry, 128), f32),
            pltpu.VMEM((ry, rx, chans, depth), f32),
            pltpu.VMEM((28, chans, 128), f32),
            pltpu.VMEM((lanes, lanes), f32),
            pltpu.VMEM((lanes, 3 * lanes), jnp.bfloat16),
            ybuf, ybuf, xbuf, xbuf, xbuf, xbuf, ybuf, ybuf,
            pltpu.VMEM((nlc * kc // 4, 16 * modes, 8 * chans), jnp.bfloat16),
            pltpu.VMEM((nlc * kc // 4, 8 * modes, chans), f32),
            dma((rx * depth // 128,)), dma((pieces,)),
            dma((pieces,)), dma((pieces,)), dma((pieces,)), dma((pieces,)),
            dma((pieces,)), dma((pieces,)), dma((pieces,)), dma((pieces,)),
            dma((4,)), dma((4,)),
        ],
        compiler_params=params(60, collective_id=0, has_side_effects=True),
        name="layer",
    )(*tables(cfg), jnp.transpose(dw_kernel, (1, 2, 3, 0)), point_weight, bias[None], field, spec_weight)
    return jax.nn.gelu(out)


def solution(mesh):
    placed = (P(None, "gx", "gy", None), P(None, None, "gx", "gy", None, None), P(), P(), P())
    return jax.shard_map(
        on_device, mesh=mesh, in_specs=placed, out_specs=P(None, "gx", "gy", None), check_vma=False
    )
```
